128 devices in a mesh: mp: 16 (over z_lo, y, core), dp: 8 (over x, z_hi).
Axes of the slice: x: 4, y: 4, z: 4 (z_hi: 2, z_lo: 2; z = z_hi * 2 + z_lo), core: 2. Of those that a mesh axis runs over, the one named last changes fastest.
Arguments:
- inputs: bfloat16 [2, 512, 13, 13, 384], P(None, 'dp'), may hold values from -6 to 6
- conv_weight: bfloat16 [2, 3, 3, 384, 256], P(None, None, None, None, 'mp'), may hold values from -0.125 to 0.125
- conv_bias: float32 [2, 256], P(None, 'mp'), may hold values from -3 to 3
- first_stitch: float32 [256, 2, 2], P('mp'), may hold values from 0.2 to 1
- fc_weight: bfloat16 [2, 9216, 4096], P(None, 'mp'), may hold values from -0.25 to 0.25
- fc_bias: float32 [4096, 2], P('mp'), may hold values from -3 to 3
- second_stitch: float32 [4096, 2, 2], P('mp'), may hold values from 0.2 to 1
- crop_counts: int32 [64], P('dp'), may hold values from 1 to 8, as said below
- out_grad: bfloat16 [4096, 2, 512], P('mp', None, 'dp'), may hold values from -6 to 6
Outputs:
- output: bfloat16 [4096, 2, 512], P('mp', None, 'dp')
- input_grad: bfloat16 [2, 512, 13, 13, 384], P(None, 'dp', None, None, 'mp')
- conv_weight_grad: float32 [2, 3, 3, 384, 256], P(None, None, None, None, 'mp')
- conv_bias_grad: float32 [2, 256], P(None, 'mp')
- first_stitch_grad: float32 [256, 2, 2], P('mp')
- fc_weight_grad: float32 [2, 9216, 4096], P(None, 'mp', 'dp')
- fc_bias_grad: float32 [4096, 2], P('mp')
- second_stitch_grad: float32 [4096, 2, 2], P('mp')
The draws below stay inside these ranges and needn't reach their ends.
Inputs may be any that keep to these rules, and one draw needn't show every extreme that they name: `crop_counts`: images of dp index d are images d * 8 onward; their crops fill that index's 64 rows from the first, the rest is padding; in every draw all images of some index hold 8 crops.
All inputs are finite; a program needn't handle non-finite values.
Results may differ from the reference program's by a relative error of at most 0.024.
Values may be sent and summed in bfloat16 or wider, within the bound.
No kernel may reach another device: no remote copies, remote signals or barrier semaphores. Data moves between devices by JAX's collectives and lax.ppermute only.
A program may use at most 192 MiB of HBM per device.

```python
import jax
import jax.numpy as jnp
from jax import lax

CIN = 384
COUT = 256
FC = 4096
MAX_CROPS = 8
IMG_DEV = 8
ROWS_DEV = 64
CROPS = 512
IMAGES = 64
N_DP = 8


def draw_crop_counts(key, part):
    key = jax.random.fold_in(key, 1)
    first_key, second_key = jax.random.split(key)
    counts = jax.random.randint(first_key, (IMAGES,), 1, MAX_CROPS + 1)
    full_owner = jax.random.randint(second_key, (), 0, IMAGES // IMG_DEV)
    owners = jnp.arange(IMAGES) // IMG_DEV
    return jnp.where(owners == full_owner, MAX_CROPS, counts).astype(jnp.int32)


def strengthened(result, key, source, target, parts, factor):
    owner, partner = [(jnp.arange(result.shape[axis_at]) // (result.shape[axis_at] // parts)).reshape([-1 if axis == axis_at else 1 for axis in range(result.ndim)]) for axis_at in (source, target)]
    chosen = jax.random.permutation(key, parts)[partner]
    strong = (owner == chosen) | (owner == (partner + parts // 2) % parts)
    return jnp.where(strong, factor * result, result)


def level_of(own_key, shape, cuts, least, largest):
    factor_of, own = 1.0, jax.random.fold_in(own_key, 6)
    for position, blocks in cuts:
        heights = jnp.exp(jax.random.uniform(jax.random.fold_in(own, position), (blocks,), jnp.float32, least / len(cuts), largest / len(cuts)))
        factor_of = factor_of * jnp.repeat(heights, shape[position] // blocks).reshape([-1 if axis == position else 1 for axis in range(len(shape))])
    return factor_of


def scatter_about(own_key, dims, deviation, limit, shards=(), kind=jnp.bfloat16):
    factor_of = level_of(own_key, dims, shards, -0.22, 0.18) if shards else 1.0
    entries = jax.random.normal(own_key, dims, jnp.float32) * deviation * factor_of
    return jnp.minimum(jnp.maximum(entries, -limit), limit).astype(kind)


def bell_draw_with(stream_key, shape, spread, most, cuts, heavy, held_as=jnp.bfloat16):
    result = spread * jax.random.normal(stream_key, shape, jnp.float32)
    if cuts:
        result = result * level_of(stream_key, shape, cuts, -0.22, 0.18)
    return jnp.clip(strengthened(result, jax.random.fold_in(stream_key, 3), *heavy), -most, most).astype(held_as)


def setup_inputs(seed: int = 0) -> dict:
    keys = jax.random.split(jax.random.key(seed), 10)
    return {
        "inputs": scatter_about(keys[0], (2, CROPS, 13, 13, CIN), 1.0, 6.0, ((1, 8),)),
        "conv_weight": bell_draw_with(keys[1], (2, 3, 3, CIN, COUT), (9 * CIN) ** -0.5, 0.125, ((4, 16),), (4, 3, 16, 2.0)),
        "conv_bias": scatter_about(keys[2], (2, COUT), 0.5, 3.0, ((1, 16),), jnp.float32),
        "first_stitch": jnp.clip(0.2 + 0.8 * jax.random.uniform(keys[3], (COUT, 2, 2), jnp.float32) ** level_of(keys[3], (COUT, 2, 2), ((0, 16),), -0.2, 0.2), 0.2, 1.0),
        "fc_weight": bell_draw_with(keys[4], (2, 36 * COUT, FC), (36 * COUT // 8) ** -0.5, 0.25, ((1, 16),), (1, 2, 16, 2.0)),
        "fc_bias": scatter_about(keys[5], (FC, 2), 0.5, 3.0, ((0, 16),), jnp.float32),
        "second_stitch": jnp.clip(0.2 + 0.8 * jax.random.uniform(keys[6], (FC, 2, 2), jnp.float32) ** level_of(keys[6], (FC, 2, 2), ((0, 16),), -0.2, 0.2), 0.2, 1.0),
        "crop_counts": draw_crop_counts(jax.random.fold_in(keys[9], 71), 0),
        "out_grad": scatter_about(keys[8], (FC, 2, CROPS), 1.0, 6.0, ((0, 16), (2, 8))),
    }


@jax.custom_vjp
def low(v):
    return lax.optimization_barrier(v.astype(jnp.bfloat16)).astype(jnp.float32)

@jax.custom_vjp
def low_back(v):
    return v

def low_keep(v):
    return (low(v), None)

def low_pass(kept, grad):
    return (grad,)

def back_keep(v):
    return (v, None)

def back_low(kept, grad):
    return (low(grad),)
low.defvjp(low_keep, low_pass)
low_back.defvjp(back_keep, back_low)
HIGH = lax.Precision.HIGHEST

def pool_matrix():
    window = jnp.arange(6)[:, None]
    cells = jnp.arange(13)[None, :]
    inside = (cells >= 2 * window) & (cells <= 2 * window + 2)
    return jnp.where(inside, 1.0 / 3.0, 0.0).astype(jnp.float32)

def forward(inputs, conv_weight, conv_bias, first_stitch, fc_weight, fc_bias, second_stitch, row_mask):
    pool_mat = pool_matrix()
    towers = []
    for tower_index in range(2):
        pre_act = lax.conv_general_dilated(inputs[tower_index], conv_weight[tower_index], (1, 1), 'SAME', dimension_numbers=('NHWC', 'HWIO', 'NHWC'), precision=HIGH)
        pre_act = low_back(pre_act + conv_bias[tower_index])
        activation = jax.nn.gelu(pre_act)
        towers.append(jnp.einsum('pi,qj,rijc->rpqc', pool_mat, pool_mat, activation, precision=HIGH))
    pooled = jnp.stack(towers)
    mixed = jnp.einsum('cuv,vrpqc->urpqc', first_stitch, pooled, precision=HIGH)
    crops = mixed.shape[1]
    flat = low(jnp.transpose(mixed, (0, 1, 4, 2, 3)).reshape(2, crops, -1))
    fc_pre = jnp.einsum('trk,tkf->ftr', flat, fc_weight, precision=HIGH) + fc_bias[:, :, None]
    hidden = jax.nn.gelu(low_back(fc_pre))
    return jnp.einsum('fuv,fvr->fur', second_stitch, hidden, precision=HIGH) * row_mask[None, None, :]

def reference(inputs, conv_weight, conv_bias, first_stitch, fc_weight, fc_bias, second_stitch, crop_counts, out_grad):
    live = lax.optimization_barrier(jnp.sum(crop_counts.reshape(N_DP, IMG_DEV), axis=1))
    rows = jnp.arange(CROPS)
    row_mask = (rows % ROWS_DEV < live[rows // ROWS_DEV]).astype(jnp.float32)
    params = (inputs.astype(jnp.float32), conv_weight.astype(jnp.float32), conv_bias, first_stitch, fc_weight.astype(jnp.float32), fc_bias, second_stitch)

    def apply(*values):
        return forward(*values, row_mask)
    output, back_fn = jax.vjp(apply, *params)
    grads = back_fn(out_grad.astype(jnp.float32))
    return (output.astype(jnp.bfloat16), grads[0].astype(jnp.bfloat16), grads[1], grads[2], grads[3], grads[4], grads[5], grads[6])
```

```python
import jax
import jax.numpy as jnp
from jax import lax
from jax.experimental import pallas as pl
from jax.experimental.pallas import tpu as pltpu
from jax.sharding import PartitionSpec as P

F32 = jnp.float32
BF16 = jnp.bfloat16
VMEM_LIMIT = 40 * 1024 * 1024


def params():
    return pltpu.CompilerParams(vmem_limit_bytes=VMEM_LIMIT)


def cost(flops, read):
    return pl.CostEstimate(flops=int(flops), bytes_accessed=int(read), transcendentals=0)


def nt_dot(left, right):
    return lax.dot_general(left, right, (((1,), (1,)), ((), ())), preferred_element_type=F32)


def nn_dot(left, right):
    return lax.dot_general(left, right, (((1,), (0,)), ((), ())), preferred_element_type=F32)


def first_half(shape):
    return lax.broadcasted_iota(jnp.int32, shape, len(shape) - 1) < 64


def swap_halves(value):
    return pltpu.roll(value, 64, value.ndim - 1)


def gelu_parts(x):
    root, cubic = 0.7978845608028654, 0.044715
    square = x * x
    tanh = jnp.tanh(root * x * (1.0 + cubic * square))
    half = 0.5 + 0.5 * tanh
    slope = half + 0.5 * x * (1.0 - tanh * tanh) * (root * (1.0 + 3.0 * cubic * square))
    return x * half, slope


def exchange(slabs, width):
    count = len(slabs)
    block = lax.broadcasted_iota(jnp.int32, slabs[0].shape, slabs[0].ndim - 1) // width
    step = 1
    while step < count:
        low = (block & step) == 0
        fresh = list(slabs)
        for p in range(count):
            if p & step == 0:
                q = p + step
                lanes = slabs[p].shape[-1]
                fresh[p] = jnp.where(low, slabs[p], pltpu.roll(slabs[q], step * width, slabs[p].ndim - 1))
                fresh[q] = jnp.where(low, pltpu.roll(slabs[p], lanes - step * width, slabs[p].ndim - 1), slabs[q])
        slabs = fresh
        step *= 2
    return slabs


def conv_kernel(x_ref, w_ref, const_ref, perm_ref, slope_ref, pooled_ref, flat_ref, flat_t_ref, acc, pool):
    i = pl.program_id(0)
    lead = first_half((16, 128))

    @pl.when(i == 0)
    def _():
        acc[...] = jnp.zeros_like(acc)
        pool[...] = jnp.zeros_like(pool)

    @pl.when(i < 13)
    def _():
        weights = w_ref[...]
        for start in range(0, 13, 2):
            width = min(2, 13 - start)
            rows = jnp.concatenate(
                [x_ref[t, 0, start + k] for k in range(width) for t in range(2)], axis=0
            )
            product = nt_dot(weights, rows)
            for k in range(width):
                lanes = slice(128 * k, 128 * k + 128)
                for a in range(3):
                    for b in range(3):
                        top = 16 * (3 * a + b)
                        term = jnp.where(
                            lead, product[top : top + 16, lanes], product[144 + top : 160 + top, lanes]
                        )
                        acc[i + 2 - a, start + k + 2 - b] += term

    @pl.when(i > 0)
    def _():
        row = i - 1
        acts = []
        for j in range(13):
            act, slope = gelu_parts(acc[i, j + 1] + const_ref[0])
            slope_ref[0, j] = slope.astype(BF16)
            acts.append(act)
        sums = [acts[2 * q] + acts[2 * q + 1] + acts[2 * q + 2] for q in range(6)]
        for q in range(6):
            pool[row // 2 + 1, q] += sums[q]

        @pl.when(row % 2 == 0)
        def _():
            for q in range(6):
                pool[row // 2, q] += sums[q]

    @pl.when(i == 13)
    def _():
        pooled = pool[1:7].reshape(36, 16, 128) * (1.0 / 9.0)
        pooled_ref[...] = pooled
        mixed = const_ref[1][None] * pooled + const_ref[2][None] * swap_halves(pooled)
        flat_t = nn_dot(perm_ref[...], mixed.reshape(576, 128).astype(BF16))
        flat_t_ref[...] = flat_t.astype(BF16)
        flat_ref[...] = flat_t.T.astype(BF16)


def conv_forward(x, w, consts, perm):
    return pl.pallas_call(
        conv_kernel,
        grid=(14,),
        in_specs=[
            pl.BlockSpec((2, 1, 13, 64, 384), lambda i: (0, jnp.minimum(i, 12), 0, 0, 0)),
            pl.BlockSpec((288, 384), lambda i: (0, 0)),
            pl.BlockSpec((4, 16, 128), lambda i: (0, 0, 0)),
            pl.BlockSpec((576, 576), lambda i: (0, 0)),
        ],
        out_specs=[
            pl.BlockSpec((1, 13, 16, 128), lambda i: (jnp.maximum(i - 1, 0), 0, 0, 0)),
            pl.BlockSpec((36, 16, 128), lambda i: (0, 0, 0)),
            pl.BlockSpec((128, 576), lambda i: (0, 0)),
            pl.BlockSpec((576, 128), lambda i: (0, 0)),
        ],
        out_shape=[
            jax.ShapeDtypeStruct((13, 13, 16, 128), BF16),
            jax.ShapeDtypeStruct((36, 16, 128), F32),
            jax.ShapeDtypeStruct((128, 576), BF16),
            jax.ShapeDtypeStruct((576, 128), BF16),
        ],
        scratch_shapes=[pltpu.VMEM((15, 15, 16, 128), F32), pltpu.VMEM((8, 6, 16, 128), F32)],
        compiler_params=params(),
        cost_estimate=cost(10e9, 20e6),
        name="conv_forward",
    )(x, w, consts, perm)


def fc_kernel(flat_ref, w_ref, out_ref):
    for t in range(2):
        product = nn_dot(flat_ref[64 * t : 64 * t + 64], w_ref[t])
        for g in range(2):
            out_ref[g, 64 * t : 64 * t + 64] = product[:, 256 * g : 256 * g + 256].astype(BF16)


def fc_forward(flat, w):
    return pl.pallas_call(
        fc_kernel,
        grid=(8,),
        in_specs=[
            pl.BlockSpec((128, 576), lambda i: (0, 0)),
            pl.BlockSpec((2, 576, 512), lambda i: (0, 0, i)),
        ],
        out_specs=pl.BlockSpec((2, 128, 256), lambda i: (i, 0, 0)),
        out_shape=jax.ShapeDtypeStruct((16, 128, 256), BF16),
        compiler_params=params(),
        cost_estimate=cost(4e9, 10e6),
        name="fc_forward",
    )(flat, w)


def hidden_kernel(counts_ref, parts_ref, bias_ref, stitch_ref, cot_ref, out_ref, grad_ref, sums_ref):
    live = counts_ref[0]
    for k in range(1, 8):
        live += counts_ref[k]
    mask = (lax.broadcasted_iota(jnp.int32, (64, 256), 0) < live).astype(F32)
    total = parts_ref[0].astype(F32)
    for k in range(1, 16):
        total += parts_ref[k].astype(F32)
    hidden, slope = [], []
    for t in range(2):
        act, der = gelu_parts(total[64 * t : 64 * t + 64] + bias_ref[t][None])
        hidden.append(act)
        slope.append(der)
    cots = [cot_ref[u].astype(F32) * mask for u in range(2)]
    stitch = [[stitch_ref[u, v][None] for v in range(2)] for u in range(2)]
    sums = []
    for u in range(2):
        out_ref[u] = (mask * (stitch[u][0] * hidden[0] + stitch[u][1] * hidden[1])).astype(BF16)
    for v in range(2):
        grad = (stitch[0][v] * cots[0] + stitch[1][v] * cots[1]) * slope[v]
        grad = grad.astype(BF16)
        for k in range(16):
            grad_ref[k, 64 * v : 64 * v + 64] = grad
        sums.append(jnp.sum(grad.astype(F32), axis=0, keepdims=True))
    for u in range(2):
        for v in range(2):
            sums.append(jnp.sum(cots[u] * hidden[v], axis=0, keepdims=True))
    sums_ref[...] = jnp.concatenate(sums + [jnp.zeros((2, 256), F32)], axis=0)


def hidden_layer(counts, parts, bias, stitch, cot):
    vmem = pl.BlockSpec(memory_space=pltpu.VMEM)
    return pl.pallas_call(
        hidden_kernel,
        in_specs=[pl.BlockSpec(memory_space=pltpu.SMEM), vmem, vmem, vmem, vmem],
        out_specs=[vmem, vmem, vmem],
        out_shape=[
            jax.ShapeDtypeStruct((2, 64, 256), BF16),
            jax.ShapeDtypeStruct((16, 128, 256), BF16),
            jax.ShapeDtypeStruct((8, 256), F32),
        ],
        compiler_params=params(),
        cost_estimate=cost(1e7, 3e6),
        name="hidden_layer",
    )(counts, parts, bias, stitch, cot)


def back_kernel(grad_ref, w_ref, perm_ref, const_ref, pooled_ref, slope_ref, send_ref, pre_ref, stats_ref, acc):
    step = pl.program_id(0)
    rows = jnp.concatenate([grad_ref[0], grad_ref[1]], axis=1)
    for t in range(2):
        product = nt_dot(w_ref[t], rows)

        @pl.when(step == 0)
        def _():
            acc[t] = product

        @pl.when(step > 0)
        def _():
            acc[t] += product

    @pl.when(step == 7)
    def _():
        flat_grad = jnp.where(first_half((576, 128)), acc[0], acc[1])
        high = flat_grad.astype(BF16)
        low = (flat_grad - high.astype(F32)).astype(BF16)
        perm = perm_ref[...]
        mixed_grad = (nn_dot(perm, high) + nn_dot(perm, low)).reshape(36, 16, 128)
        pooled = pooled_ref[...]
        lead = first_half((16, 128))
        own = jnp.sum(mixed_grad * pooled, axis=0)
        cross = jnp.sum(mixed_grad * swap_halves(pooled), axis=0)
        pooled_grad = const_ref[1][None] * mixed_grad + const_ref[3][None] * swap_halves(mixed_grad)
        pooled_grad = (pooled_grad * (1.0 / 9.0)).reshape(6, 6, 16, 128)
        bias_sum = jnp.zeros((16, 128), F32)
        zero = jnp.zeros((16, 128), F32)
        spread = []
        for p in range(6):
            line = []
            for j in range(13):
                terms = [pooled_grad[p, q] for q in range(6) if 2 * q <= j <= 2 * q + 2]
                line.append(terms[0] if len(terms) == 1 else terms[0] + terms[1])
            spread.append(line)
        for i in range(13):
            windows = [p for p in range(6) if 2 * p <= i <= 2 * p + 2]
            slabs = []
            for j in range(13):
                value = spread[windows[0]][j]
                if len(windows) == 2:
                    value = value + spread[windows[1]][j]
                value = (value * slope_ref[i, j].astype(F32)).astype(BF16)
                pre_ref[i, j] = value
                value = value.astype(F32)
                bias_sum = bias_sum + value
                slabs.append(value)
            slabs = exchange(slabs + [zero] * 3, 8)
            for m in range(16):
                block = (m % 2) * 8 + m // 2
                send_ref[m, :, 128 * i : 128 * i + 128] = slabs[block].astype(BF16)
        lane = lax.broadcasted_iota(jnp.int32, (16, 128), 1)
        stats = jnp.zeros((16, 128), F32)
        for k, value in enumerate((own, cross, bias_sum)):
            for t in range(2):
                half = jnp.sum(jnp.where(lead == (t == 0), value, 0.0), axis=1, keepdims=True)
                stats = jnp.where(lane == 2 * k + t, half, stats)
        stats_ref[...] = stats


def back_fc(grads, w, perm, consts, pooled, slope):
    whole = lambda *shape: pl.BlockSpec(shape, lambda i: (0,) * len(shape))
    return pl.pallas_call(
        back_kernel,
        grid=(8,),
        in_specs=[
            pl.BlockSpec((2, 128, 256), lambda i: (i, 0, 0)),
            pl.BlockSpec((2, 576, 512), lambda i: (0, 0, i)),
            whole(576, 576),
            whole(4, 16, 128),
            whole(36, 16, 128),
            whole(13, 13, 16, 128),
        ],
        out_specs=[whole(16, 16, 1664), whole(13, 13, 16, 128), whole(16, 128)],
        out_shape=[
            jax.ShapeDtypeStruct((16, 16, 1664), BF16),
            jax.ShapeDtypeStruct((13, 13, 16, 128), BF16),
            jax.ShapeDtypeStruct((16, 128), F32),
        ],
        scratch_shapes=[pltpu.VMEM((2, 576, 128), F32)],
        compiler_params=params(),
        cost_estimate=cost(4e9, 12e6),
        name="back_fc",
    )(grads, w, perm, consts, pooled, slope)


def weight_kernel(x_ref, pre_ref, sums_ref, stats_ref, out_ref, parts, acc):
    i = pl.program_id(0)

    @pl.when(i == 0)
    def _():
        parts[...] = jnp.zeros_like(parts)
        lead = first_half((13, 13, 16, 128))
        value = pre_ref[...]
        none = jnp.zeros_like(value)
        parts[0, 1:14, 1:14] = jnp.where(lead, value, none)
        parts[1, 1:14, 1:14] = jnp.where(lead, none, value)

    left = jnp.concatenate(
        [
            jnp.concatenate([parts[t, i + 2 - a, j + 2 - b] for j in range(13)], axis=1)
            for t in range(2)
            for a in range(3)
            for b in range(3)
        ],
        axis=0,
    )
    right = jnp.concatenate([x_ref[t, 0, j] for j in range(13) for t in range(2)], axis=0)
    product = nn_dot(left, right)

    @pl.when(i == 0)
    def _():
        acc[...] = product

    @pl.when(i > 0)
    def _():
        acc[...] += product

    @pl.when(i == 12)
    def _():
        out_ref[0:288] = acc[...].astype(BF16)
        small = jnp.concatenate([sums_ref[...], jnp.zeros((8, 256), F32)], axis=0)
        out_ref[288:304] = jnp.concatenate([small, stats_ref[...]], axis=1).astype(BF16)


def weight_grad(x, pre, sums, stats):
    whole = lambda *shape: pl.BlockSpec(shape, lambda i: (0,) * len(shape))
    return pl.pallas_call(
        weight_kernel,
        grid=(13,),
        in_specs=[
            pl.BlockSpec((2, 1, 13, 64, 384), lambda i: (0, i, 0, 0, 0)),
            whole(13, 13, 16, 128),
            whole(8, 256),
            whole(16, 128),
        ],
        out_specs=whole(304, 384),
        out_shape=jax.ShapeDtypeStruct((304, 384), BF16),
        scratch_shapes=[pltpu.VMEM((2, 15, 15, 16, 128), BF16), pltpu.VMEM((288, 384), F32)],
        compiler_params=params(),
        cost_estimate=cost(10e9, 20e6),
        name="weight_grad",
    )(x, pre, sums, stats)


def turn_kernel(w_ref, out_ref):
    for tap in range(9):
        rows = w_ref[:, 16 * tap : 16 * tap + 16].reshape(256, 384)
        out_ref[:, 256 * tap : 256 * tap + 256] = rows.T


def turned(w):
    return pl.pallas_call(
        turn_kernel,
        out_shape=jax.ShapeDtypeStruct((384, 2304), BF16),
        compiler_params=params(),
        cost_estimate=cost(1e9, 4e6),
        name="turned_kernels",
    )(w)


def input_kernel(g_ref, w_ref, out_ref, taps):
    g = g_ref[...].reshape(256, 1664).astype(F32)
    zero = jnp.zeros((256, 128), BF16)
    for b in range(3):
        taps[b, :, 0:128] = zero
        taps[b, :, 1792:1920] = zero
        for i in range(13):
            row = g[:, 128 * i : 128 * i + 128]
            if b == 0:
                row = pltpu.roll(row, 120, 1)
            if b == 2:
                row = pltpu.roll(row, 8, 1)
            taps[b, :, 128 * i + 128 : 128 * i + 256] = row.astype(BF16)
    weights = w_ref[...]
    for start in range(0, 13, 2):
        width = 128 * min(2, 13 - start)
        right = jnp.concatenate(
            [
                taps[b, :, 128 * (start + 2 - a) : 128 * (start + 2 - a) + width]
                for a in range(3)
                for b in range(3)
            ],
            axis=0,
        )
        product = nn_dot(weights, right)
        for m in range(16):
            out_ref[m, :, 128 * start : 128 * start + width] = product[24 * m : 24 * m + 24].astype(BF16)


def input_grad_part(g, w):
    return pl.pallas_call(
        input_kernel,
        out_shape=jax.ShapeDtypeStruct((16, 24, 1664), BF16),
        scratch_shapes=[pltpu.VMEM((3, 256, 1920), BF16)],
        compiler_params=params(),
        cost_estimate=cost(4e9, 4e6),
        name="input_grad",
    )(g, w)


def place_kernel(part_ref, out_ref):
    slabs = [part_ref[2 * (block % 8) + block // 8].astype(F32) for block in range(16)]
    slabs = exchange(slabs, 8)
    for j in range(13):
        out_ref[0, 0, j] = slabs[j][:, 0:64].astype(BF16)
        out_ref[1, 0, j] = swap_halves(slabs[j])[:, 0:64].astype(BF16)


def placed_back(parts):
    return pl.pallas_call(
        place_kernel,
        grid=(13,),
        in_specs=[pl.BlockSpec((16, 24, 128), lambda i: (0, 0, i))],
        out_specs=pl.BlockSpec((2, 1, 13, 24, 64), lambda i: (0, i, 0, 0, 0)),
        out_shape=jax.ShapeDtypeStruct((2, 13, 13, 24, 64), BF16),
        compiler_params=params(),
        cost_estimate=cost(1e8, 3e6),
        name="placed_back",
    )(parts)


def fc_weight_kernel(flat_ref, grad_ref, out_ref):
    t = pl.program_id(0)
    lead = first_half((576, 128)) == (t == 0)
    zero = jnp.zeros((576, 128), BF16)
    left = jnp.concatenate([jnp.where(lead, flat_ref[d], zero) for d in range(8)], axis=1)
    for g in range(2):
        right = jnp.concatenate([grad_ref[d, g] for d in range(8)], axis=0)
        out_ref[0, :, 256 * g : 256 * g + 256] = nn_dot(left, right)


def fc_weight_grad_of(flats, grads):
    return pl.pallas_call(
        fc_weight_kernel,
        grid=(2,),
        in_specs=[
            pl.BlockSpec((8, 576, 128), lambda t: (0, 0, 0)),
            pl.BlockSpec((8, 2, 128, 256), lambda t: (0, 0, 0, 0)),
        ],
        out_specs=pl.BlockSpec((1, 576, 512), lambda t: (t, 0, 0)),
        out_shape=jax.ShapeDtypeStruct((2, 576, 512), F32),
        compiler_params=params(),
        cost_estimate=cost(3e9, 5e6),
        name="fc_weight_grad",
    )(flats, grads)


def total_kernel(parts_ref, conv_ref, sums_ref, stats_ref):
    total = parts_ref[0].astype(F32)
    for k in range(1, 8):
        total += parts_ref[k].astype(F32)
    conv_ref[...] = total[0:288]
    sums_ref[...] = total[288:296, 0:256]
    stats_ref[...] = total[288:304, 256:384]


def summed(parts):
    return pl.pallas_call(
        total_kernel,
        out_shape=[
            jax.ShapeDtypeStruct((288, 384), F32),
            jax.ShapeDtypeStruct((8, 256), F32),
            jax.ShapeDtypeStruct((16, 128), F32),
        ],
        compiler_params=params(),
        cost_estimate=cost(1e7, 3e6),
        name="summed",
    )(parts)


def dealt(array, axis):
    return lax.all_to_all(array, axis, 0, 0, tiled=True)


def copies(array, count):
    return jnp.broadcast_to(array[None], (count, *array.shape))


def local(
    inputs,
    conv_weight,
    conv_bias,
    first_stitch,
    fc_weight,
    fc_bias,
    second_stitch,
    crop_counts,
    out_grad,
):
    x = jnp.transpose(inputs, (0, 2, 3, 1, 4))
    kernels = jnp.transpose(conv_weight, (0, 1, 2, 4, 3)).reshape(2, 144, 384)

    fc_row = jnp.arange(576)
    slab_row = (fc_row % 36) * 16 + fc_row // 36
    perm = (slab_row[:, None] == fc_row[None, :]).astype(BF16)
    perm_back = (slab_row[None, :] == fc_row[:, None]).astype(BF16)

    def lanes(pair):
        return jnp.repeat(pair, 64, axis=1)

    own = jnp.stack([first_stitch[:, 0, 0], first_stitch[:, 1, 1]], axis=1)
    consts = jnp.stack(
        [
            lanes(conv_bias.T),
            lanes(own),
            lanes(jnp.stack([first_stitch[:, 0, 1], first_stitch[:, 1, 0]], axis=1)),
            lanes(jnp.stack([first_stitch[:, 1, 0], first_stitch[:, 0, 1]], axis=1)),
        ]
    )

    slope, pooled, flat, flat_t = conv_forward(x, kernels.reshape(288, 384), consts, perm)
    parts = dealt(fc_forward(flat, fc_weight), "mp")
    output, grad_copies, sums = hidden_layer(
        crop_counts,
        parts,
        fc_bias.T,
        jnp.transpose(second_stitch, (1, 2, 0)),
        jnp.transpose(out_grad, (1, 2, 0)),
    )
    grads = dealt(grad_copies, "mp")
    send, pre, stats = back_fc(grads, fc_weight, perm_back, consts, pooled, slope)
    pre_all = dealt(send, "mp")

    kernels_all = turned(dealt(jnp.tile(kernels, (8, 1, 1)), "mp"))
    part = dealt(input_grad_part(pre_all, kernels_all), "mp")
    input_grad = jnp.transpose(placed_back(part), (0, 4, 1, 2, 3))

    gathered = dealt(copies(weight_grad(x, pre, sums, stats), 8), "dp")
    conv_sum, f_sums, c_sums = summed(gathered)
    flats = dealt(copies(flat_t, 8), "dp")
    grads_dp = dealt(grads.reshape(8, 2, 128, 256), "dp")
    fc_weight_grad = fc_weight_grad_of(flats, grads_dp)

    conv_weight_grad = jnp.transpose(conv_sum.reshape(2, 3, 3, 16, 384), (0, 1, 2, 4, 3))
    first_stitch_grad = jnp.stack(
        [
            jnp.stack([c_sums[:, 0], c_sums[:, 2]], axis=1),
            jnp.stack([c_sums[:, 3], c_sums[:, 1]], axis=1),
        ],
        axis=1,
    )
    conv_bias_grad = c_sums[:, 4:6].T
    fc_bias_grad = f_sums[0:2].T
    second_stitch_grad = jnp.transpose(f_sums[2:6].reshape(2, 2, 256), (2, 0, 1))
    return (
        jnp.transpose(output, (2, 0, 1)),
        input_grad,
        conv_weight_grad,
        conv_bias_grad,
        first_stitch_grad,
        fc_weight_grad,
        fc_bias_grad,
        second_stitch_grad,
    )


def solution(mesh):
    placed = (
        P(None, "dp", None, None, None),
        P(None, None, None, None, "mp"),
        P(None, "mp"),
        P("mp", None, None),
        P(None, "mp", None),
        P("mp", None),
        P("mp", None, None),
        P("dp"),
        P("mp", None, "dp"),
    )
    return jax.shard_map(
        local,
        mesh=mesh,
        in_specs=placed,
        out_specs=(
            P("mp", None, "dp"),
            P(None, "dp", None, None, "mp"),
            P(None, None, None, None, "mp"),
            P(None, "mp"),
            P("mp", None, None),
            P(None, "mp", "dp"),
            P("mp", None),
            P("mp", None, None),
        ),
        check_vma=False,
    )
```

```python
import jax
import jax.numpy as jnp
from jax import lax
from jax.experimental import pallas as pl
from jax.experimental.pallas import tpu as pltpu
from jax.sharding import PartitionSpec as P

F32 = jnp.float32
BF16 = jnp.bfloat16
LARGE, SMALL = 58, 16


def params(mib=LARGE):
    return pltpu.CompilerParams(vmem_limit_bytes=mib * 1024 * 1024)


def cost(flops, read):
    return pl.CostEstimate(flops=int(flops), bytes_accessed=int(read), transcendentals=0)


def nt_dot(left, right):
    return lax.dot_general(left, right, (((1,), (1,)), ((), ())), preferred_element_type=F32)


def nn_dot(left, right):
    return lax.dot_general(left, right, (((1,), (0,)), ((), ())), preferred_element_type=F32)


def first_half(shape):
    return lax.broadcasted_iota(jnp.int32, shape, len(shape) - 1) < 64


def swap_halves(value):
    return pltpu.roll(value, 64, value.ndim - 1)


def gelu_parts(x):
    root, cubic = 0.7978845608028654, 0.044715
    square = x * x
    tanh = jnp.tanh(root * x * (1.0 + cubic * square))
    half = 0.5 + 0.5 * tanh
    slope = half + 0.5 * x * (1.0 - tanh * tanh) * (root * (1.0 + 3.0 * cubic * square))
    return x * half, slope


def spread(slabs):
    lane = lax.broadcasted_iota(jnp.int32, slabs[0].shape, 1)
    for bit in range(4):
        odd = (lane & (8 << bit)) != 0
        slabs = [jnp.where(odd, slabs[(k + (1 << bit)) % 16], slabs[k]) for k in range(16)]
    return slabs


def exchange(slabs):
    slabs = spread(slabs)
    slabs = [slabs[0]] + [pltpu.roll(slabs[k], 8 * k, 1) for k in range(1, 16)]
    slabs = spread(slabs)
    return [slabs[-k % 16] for k in range(16)]


def column(row):
    size = row.shape[1]
    eye = lax.broadcasted_iota(jnp.int32, (size, size), 0) == lax.broadcasted_iota(jnp.int32, (size, size), 1)
    return jnp.sum(jnp.where(eye, row, 0.0), axis=1, keepdims=True)


def by_tower(first, second):
    lead = first_half((16, 128))
    return jnp.where(lead, column(first), column(second))


def stitch_slabs(stitch_ref):
    part = [[stitch_ref[u, v : v + 1] for v in range(2)] for u in range(2)]
    own = by_tower(part[0][0], part[1][1])
    into = by_tower(part[0][1], part[1][0])
    back = by_tower(part[1][0], part[0][1])
    return own, into, back


def slab_order(fc_axis):
    fc_row = lax.broadcasted_iota(jnp.int32, (576, 576), fc_axis)
    slab_row = lax.broadcasted_iota(jnp.int32, (576, 576), 1 - fc_axis)
    return (fc_row == 36 * (slab_row & 15) + (slab_row >> 4)).astype(F32).astype(BF16)


def front_kernel(
    core_ref, x_ref, w_ref, kernel_ref, bias_ref, stitch_ref,
    slope_ref, pooled_ref, flat_t_ref, own_ref, other_ref,
    xs, ws, acc, ready, pool, slopes, pooled_out, flat_t_out, parts, x_sem, w_sem, slope_sem, out_sem,
):
    def x_copy(i):
        return pltpu.make_async_copy(x_ref.at[:, i], xs.at[:, i], x_sem.at[i])

    def w_copy(t):
        return pltpu.make_async_copy(w_ref.at[t], ws.at[t], w_sem.at[t])

    def slope_copy(i):
        return pltpu.make_async_copy(slopes.at[i], slope_ref.at[i], slope_sem.at[i])

    for i in range(13):
        x_copy(i).start()
    for t in range(2):
        w_copy(t).start()
    acc[...] = jnp.zeros_like(acc)
    ready[...] = jnp.zeros_like(ready)
    pool[...] = jnp.zeros_like(pool)
    lead = first_half((16, 128))
    bias = by_tower(bias_ref[0:1], bias_ref[1:2])
    own, into, _ = stitch_slabs(stitch_ref)

    def gather(row):
        for t in range(2):
            right = pltpu.roll(acc[t, 0, row + 1], 64, 1)
            left = pltpu.roll(acc[t, 2, row + 1], 832, 1)
            ready[t] = acc[t, 1, row + 1] + right + left

    def finish(row):
        acts = []
        for j in range(13):
            lanes = slice(j // 2 * 128, j // 2 * 128 + 128)
            zero, one = ready[0, :, lanes], ready[1, :, lanes]
            if j % 2 == 0:
                pre_act = jnp.where(lead, zero, swap_halves(one))
            else:
                pre_act = jnp.where(lead, swap_halves(zero), one)
            act, slope = gelu_parts(pre_act + bias)
            slopes[jnp.maximum(row, 0), j] = slope.astype(BF16)
            acts.append(act)
        even = row % 2 == 0
        for q in range(6):
            total = acts[2 * q] + acts[2 * q + 1] + acts[2 * q + 2]
            pool[(row + 2) // 2, q] += total
            pool[jnp.maximum(row, 0) // 2, q] += jnp.where(even, total, 0.0)

    def line(i, carry):
        x_copy(i).wait()
        finish(i - 2)
        for t in range(2):
            weights = kernel_ref[144 * t : 144 * t + 144]
            for start in range(0, 13, 4):
                width = min(4, 13 - start)
                rows = xs[t, i, start : start + width].reshape(64 * width, 384)
                product = nt_dot(weights, rows)
                for a in range(3):
                    for b in range(3):
                        top = 16 * (3 * a + b)
                        acc[t, b, i + 2 - a, :, 64 * start : 64 * (start + width)] += product[top : top + 16]
        gather(i - 1)
        return carry

    def last(i, carry):
        finish(i - 2)
        gather(jnp.minimum(i - 1, 12))
        return carry

    lax.fori_loop(0, 13, line, 0)
    lax.fori_loop(13, 15, last, 0)
    for i in range(13):
        slope_copy(i).start()
    pooled = pool[1:7].reshape(36, 16, 128) * (1.0 / 9.0)
    pooled_out[...] = pooled
    pooled_copy = pltpu.make_async_copy(pooled_out, pooled_ref, out_sem.at[0])
    pooled_copy.start()
    mixed = own[None] * pooled + into[None] * swap_halves(pooled)
    flat_t = nn_dot(slab_order(0), mixed.reshape(576, 128).astype(BF16))
    flat_t_out[...] = flat_t.astype(BF16)
    flat_copy = pltpu.make_async_copy(flat_t_out, flat_t_ref, out_sem.at[1])
    flat_copy.start()
    flat = flat_t.T.astype(BF16)
    core = core_ref[0]
    copies_out = [pooled_copy, flat_copy]
    for t in range(2):
        w_copy(t).wait()
    for k, (ref, parity) in enumerate(((other_ref, 1 - core), (own_ref, core))):
        for q in range(8):
            at = pl.ds(pl.multiple_of((2 * q + parity) * 256, 256), 256)
            for t in range(2):
                parts[k, q, 64 * t : 64 * t + 64] = nn_dot(flat[64 * t : 64 * t + 64], ws[t, :, at]).astype(BF16)
            if q % 4 == 3:
                some = pl.ds(q - 3, 4)
                copy = pltpu.make_async_copy(parts.at[k, some], ref.at[some], out_sem.at[2 + 2 * k + q // 4])
                copy.start()
                copies_out.append(copy)
    for i in range(13):
        slope_copy(i).wait()
    for copy in copies_out:
        copy.wait()


VMEM = pl.BlockSpec(memory_space=pltpu.VMEM)
SMEM = pl.BlockSpec(memory_space=pltpu.SMEM)
ANY = pl.BlockSpec(memory_space=pl.ANY)


def front(core, x, w, kernels, bias, stitch):
    return pl.pallas_call(
        front_kernel,
        in_specs=[SMEM, ANY, ANY, VMEM, VMEM, VMEM],
        out_specs=[ANY] * 5,
        out_shape=[
            jax.ShapeDtypeStruct((13, 13, 16, 128), BF16),
            jax.ShapeDtypeStruct((36, 16, 128), F32),
            jax.ShapeDtypeStruct((576, 128), BF16),
            jax.ShapeDtypeStruct((8, 128, 256), BF16),
            jax.ShapeDtypeStruct((8, 128, 256), BF16),
        ],
        scratch_shapes=[
            pltpu.VMEM((2, 13, 13, 64, 384), BF16),
            pltpu.VMEM((2, 576, 4096), BF16),
            pltpu.VMEM((2, 3, 15, 16, 896), F32),
            pltpu.VMEM((2, 16, 896), F32),
            pltpu.VMEM((8, 6, 16, 128), F32),
            pltpu.VMEM((13, 13, 16, 128), BF16),
            pltpu.VMEM((36, 16, 128), F32),
            pltpu.VMEM((576, 128), BF16),
            pltpu.VMEM((2, 8, 128, 256), BF16),
            pltpu.SemaphoreType.DMA((13,)),
            pltpu.SemaphoreType.DMA((2,)),
            pltpu.SemaphoreType.DMA((13,)),
            pltpu.SemaphoreType.DMA((6,)),
        ],
        compiler_params=params(),
        cost_estimate=cost(10e9, 30e6),
        name="front",
    )(core, x, w, kernels, bias, stitch)


def hidden_kernel(counts_ref, parts_ref, bias_ref, stitch_ref, cot_ref, out_ref, grad_ref, sums_ref):
    live = counts_ref[0]
    for k in range(1, 8):
        live += counts_ref[k]
    mask = (lax.broadcasted_iota(jnp.int32, (64, 256), 0) < live).astype(F32)
    total = parts_ref[0].astype(F32)
    for k in range(1, 8):
        total += parts_ref[k].astype(F32)
    hidden, slope = [], []
    for t in range(2):
        act, der = gelu_parts(total[64 * t : 64 * t + 64] + bias_ref[t][None])
        hidden.append(act)
        slope.append(der)
    cots = [cot_ref[u].astype(F32) * mask for u in range(2)]
    stitch = [[stitch_ref[u, v][None] for v in range(2)] for u in range(2)]
    sums = []
    for u in range(2):
        out_ref[u] = (mask * (stitch[u][0] * hidden[0] + stitch[u][1] * hidden[1])).astype(BF16)
    for v in range(2):
        grad = (stitch[0][v] * cots[0] + stitch[1][v] * cots[1]) * slope[v]
        grad = grad.astype(BF16)
        for k in range(8):
            for half in range(2):
                top = 128 * half + 64 * v
                grad_ref[k, top : top + 64] = grad[:, 128 * half : 128 * half + 128]
        sums.append(jnp.sum(grad.astype(F32), axis=0, keepdims=True))
    for u in range(2):
        for v in range(2):
            sums.append(jnp.sum(cots[u] * hidden[v], axis=0, keepdims=True))
    sums_ref[...] = jnp.concatenate(sums + [jnp.zeros((2, 256), F32)], axis=0)


def hidden_layer(counts, parts, bias, stitch, cot):
    vmem = pl.BlockSpec(memory_space=pltpu.VMEM)
    return pl.pallas_call(
        hidden_kernel,
        in_specs=[pl.BlockSpec(memory_space=pltpu.SMEM), vmem, vmem, vmem, vmem],
        out_specs=[vmem, vmem, vmem],
        out_shape=[
            jax.ShapeDtypeStruct((2, 64, 256), BF16),
            jax.ShapeDtypeStruct((8, 256, 128), BF16),
            jax.ShapeDtypeStruct((8, 256), F32),
        ],
        compiler_params=params(SMALL),
        cost_estimate=cost(1e7, 3e6),
        name="hidden_layer",
    )(counts, parts, bias, stitch, cot)


def back_kernel(
    core_ref, own_ref, other_ref, w_ref, stitch_ref, pooled_ref, slope_ref,
    send_ref, pre_ref, stats_ref,
    ws, grads, pooled, slopes, sends, pres, w_sem, in_sem, send_sem, pre_sem,
):
    def w_copy(k):
        at = pl.ds(1024 * k, 1024)
        return pltpu.make_async_copy(w_ref.at[:, :, at], ws.at[:, :, at], w_sem.at[k])

    first_in = [
        pltpu.make_async_copy(own_ref, grads.at[0], in_sem.at[0]),
        pltpu.make_async_copy(other_ref, grads.at[1], in_sem.at[1]),
    ]
    later_in = [
        pltpu.make_async_copy(pooled_ref, pooled, in_sem.at[2]),
        pltpu.make_async_copy(slope_ref, slopes, in_sem.at[3]),
    ]
    for copy in first_in:
        copy.start()
    for k in range(4):
        w_copy(k).start()
    for copy in later_in:
        copy.start()
    first = core_ref[0] == 0
    perm = slab_order(1)
    own_slab, _, back_slab = stitch_slabs(stitch_ref)
    for copy in first_in:
        copy.wait()
    totals = [jnp.zeros((576, 128), F32)] * 2
    for k in range(4):
        w_copy(k).wait()
        blocks = []
        for q in (2 * k, 2 * k + 1):
            own, other = (jnp.concatenate([grads[p, q, 0:128], grads[p, q, 128:256]], axis=1) for p in range(2))
            blocks += [jnp.where(first, own, other), jnp.where(first, other, own)]
        rows = jnp.concatenate(blocks, axis=1)
        for t in range(2):
            totals[t] = totals[t] + nt_dot(ws[t, :, 1024 * k : 1024 * k + 1024], rows)
    flat_grad = jnp.where(first_half((576, 128)), totals[0], totals[1])
    high = flat_grad.astype(BF16)
    low = (flat_grad - high.astype(F32)).astype(BF16)
    mixed_grad = (nn_dot(perm, high) + nn_dot(perm, low)).reshape(36, 16, 128)
    swapped = swap_halves(mixed_grad)
    pooled_grad = own_slab[None] * mixed_grad + back_slab[None] * swapped
    pooled_grad = (pooled_grad * (1.0 / 9.0)).reshape(6, 6, 16, 128)
    for copy in later_in:
        copy.wait()
    lead = first_half((16, 128))
    bias_sum = jnp.zeros((16, 128), F32)
    zero = jnp.zeros((16, 128), F32)
    widened = []
    for p in range(6):
        line = []
        for j in range(13):
            terms = [pooled_grad[p, q] for q in range(6) if 2 * q <= j <= 2 * q + 2]
            line.append(terms[0] if len(terms) == 1 else terms[0] + terms[1])
        widened.append(line)
    copies_out = []
    for i in range(13):
        windows = [p for p in range(6) if 2 * p <= i <= 2 * p + 2]
        slabs = []
        for j in range(13):
            value = widened[windows[0]][j]
            if len(windows) == 2:
                value = value + widened[windows[1]][j]
            value = (value * slopes[i, j].astype(F32)).astype(BF16)
            pres[i, j] = value
            value = value.astype(F32)
            bias_sum = bias_sum + value
            slabs.append(value)
        slabs = exchange(slabs + [zero] * 3)
        at = pl.ds(128 * i, 128)
        for m in range(16):
            block = (m % 2) * 8 + m // 2
            sends[m, :, 128 * i : 128 * i + 128] = slabs[block].astype(BF16)
        copies_out.append(pltpu.make_async_copy(sends.at[:, :, at], send_ref.at[:, :, at], send_sem.at[i]))
        copies_out[-1].start()
        copies_out.append(pltpu.make_async_copy(pres.at[i], pre_ref.at[i], pre_sem.at[i]))
        copies_out[-1].start()
    pooled_in = pooled[...]
    own = jnp.sum(mixed_grad * pooled_in, axis=0)
    cross = jnp.sum(swapped * pooled_in, axis=0)
    lane = lax.broadcasted_iota(jnp.int32, (16, 128), 1)
    stats = jnp.zeros((16, 128), F32)
    for k, value in enumerate((own, cross, bias_sum)):
        for t in range(2):
            half = jnp.sum(jnp.where(lead == (t == 0), value, 0.0), axis=1, keepdims=True)
            stats = jnp.where(lane == 2 * k + t, half, stats)
    stats_ref[...] = stats
    for copy in copies_out:
        copy.wait()


def back_fc(core, own, other, w, stitch, pooled, slope):
    return pl.pallas_call(
        back_kernel,
        in_specs=[SMEM, ANY, ANY, ANY, VMEM, ANY, ANY],
        out_specs=[ANY, ANY, VMEM],
        out_shape=[
            jax.ShapeDtypeStruct((16, 16, 1664), BF16),
            jax.ShapeDtypeStruct((13, 13, 16, 128), BF16),
            jax.ShapeDtypeStruct((16, 128), F32),
        ],
        scratch_shapes=[
            pltpu.VMEM((2, 576, 4096), BF16),
            pltpu.VMEM((2, 8, 256, 128), BF16),
            pltpu.VMEM((36, 16, 128), F32),
            pltpu.VMEM((13, 13, 16, 128), BF16),
            pltpu.VMEM((16, 16, 1664), BF16),
            pltpu.VMEM((13, 13, 16, 128), BF16),
            pltpu.SemaphoreType.DMA((4,)),
            pltpu.SemaphoreType.DMA((4,)),
            pltpu.SemaphoreType.DMA((13,)),
            pltpu.SemaphoreType.DMA((13,)),
        ],
        compiler_params=params(),
        cost_estimate=cost(1e8, 1e6),
        name="back_fc",
    )(core, own, other, w, stitch, pooled, slope)


def weight_kernel(x_ref, pre_ref, sums_ref, stats_ref, out_ref, xs, lines, acc, x_sem):
    def x_copy(i):
        return pltpu.make_async_copy(x_ref.at[:, i], xs.at[:, i], x_sem.at[i])

    for i in range(13):
        x_copy(i).start()
    lines[...] = jnp.zeros_like(lines)
    acc[...] = jnp.zeros_like(acc)
    lead = first_half((16, 128))

    def merge(i, carry):
        zero = jnp.zeros((16, 128), F32)
        slabs = [pre_ref[i, j].astype(F32) for j in range(13)]
        turned = [swap_halves(slab) for slab in slabs]
        slabs = [zero] + slabs + [zero] * 2
        turned = [zero] + turned + [zero] * 2
        for first in range(-1, 14):
            left, right = first + 1, first + 2
            pair = (
                jnp.where(lead, slabs[left], turned[right]).astype(BF16),
                jnp.where(lead, turned[left], slabs[right]).astype(BF16),
            )
            for b in range(3):
                place = first + b - 1
                if place % 2 == 0 and 0 <= place <= 12:
                    for t in range(2):
                        lines[t, b, i + 1, :, 64 * place : 64 * place + 128] = pair[t]
        return carry

    lax.fori_loop(0, 13, merge, 0)

    def line(i, carry):
        x_copy(i).wait()
        for t in range(2):
            left = jnp.concatenate([lines[t, b, i + 2 - a] for a in range(3) for b in range(3)], axis=0)
            right = jnp.concatenate([xs[t, i].reshape(832, 384), jnp.zeros((64, 384), BF16)], axis=0)
            acc[144 * t : 144 * t + 144] += nn_dot(left, right)
        return carry

    lax.fori_loop(0, 13, line, 0)
    out_ref[0:288] = acc[...].astype(BF16)
    small = jnp.concatenate([sums_ref[...], jnp.zeros((8, 256), F32)], axis=0)
    out_ref[288:304] = jnp.concatenate([small, stats_ref[...]], axis=1).astype(BF16)


def weight_grad(x, pre, sums, stats):
    return pl.pallas_call(
        weight_kernel,
        in_specs=[ANY, VMEM, VMEM, VMEM],
        out_specs=VMEM,
        out_shape=jax.ShapeDtypeStruct((304, 384), BF16),
        scratch_shapes=[
            pltpu.VMEM((2, 13, 13, 64, 384), BF16),
            pltpu.VMEM((2, 3, 15, 16, 896), BF16),
            pltpu.VMEM((288, 384), F32),
            pltpu.SemaphoreType.DMA((13,)),
        ],
        compiler_params=params(),
        cost_estimate=cost(10e9, 20e6),
        name="weight_grad",
    )(x, pre, sums, stats)


def turn_kernel(core_ref, blocks_ref, out_ref, rows):
    core = core_ref[0]
    for k in range(8):
        for p, parity in ((0, core), (1, 1 - core)):
            at = pl.ds(pl.multiple_of(16 * (2 * k + parity), 16), 16)
            for tap in range(9):
                rows[tap, at] = blocks_ref[k, p, 16 * tap : 16 * tap + 16]
    for tap in range(9):
        out_ref[:, 256 * tap : 256 * tap + 256] = rows[tap].T


def turned(core, blocks):
    return pl.pallas_call(
        turn_kernel,
        in_specs=[SMEM, VMEM],
        out_specs=VMEM,
        out_shape=jax.ShapeDtypeStruct((384, 2304), BF16),
        scratch_shapes=[pltpu.VMEM((9, 256, 384), BF16)],
        compiler_params=params(SMALL),
        cost_estimate=cost(1e9, 4e6),
        name="turned_kernels",
    )(core, blocks)


def input_kernel(g_ref, w_ref, out_ref, taps):
    g = g_ref[...].reshape(256, 1664).astype(F32)
    zero = jnp.zeros((256, 128), BF16)
    for b in range(3):
        taps[b, :, 0:128] = zero
        taps[b, :, 1792:1920] = zero
        for i in range(13):
            row = g[:, 128 * i : 128 * i + 128]
            if b == 0:
                row = pltpu.roll(row, 120, 1)
            if b == 2:
                row = pltpu.roll(row, 8, 1)
            taps[b, :, 128 * i + 128 : 128 * i + 256] = row.astype(BF16)
    weights = w_ref[...]
    for start in range(0, 13, 2):
        width = 128 * min(2, 13 - start)
        right = jnp.concatenate(
            [
                taps[b, :, 128 * (start + 2 - a) : 128 * (start + 2 - a) + width]
                for a in range(3)
                for b in range(3)
            ],
            axis=0,
        )
        product = nn_dot(weights, right)
        for m in range(16):
            out_ref[m, :, 128 * start : 128 * start + width] = product[24 * m : 24 * m + 24].astype(BF16)


def input_grad_part(g, w):
    return pl.pallas_call(
        input_kernel,
        in_specs=[VMEM, VMEM],
        out_specs=VMEM,
        out_shape=jax.ShapeDtypeStruct((16, 24, 1664), BF16),
        scratch_shapes=[pltpu.VMEM((3, 256, 1920), BF16)],
        compiler_params=params(SMALL),
        cost_estimate=cost(4e9, 4e6),
        name="input_grad",
    )(g, w)


def place_kernel(part_ref, out_ref):
    for i in range(13):
        lanes = slice(128 * i, 128 * i + 128)
        slabs = [part_ref[2 * (block % 8) + block // 8, :, lanes].astype(F32) for block in range(16)]
        slabs = exchange(slabs)
        for j in range(13):
            out_ref[0, i, j] = slabs[j][:, 0:64].astype(BF16)
            out_ref[1, i, j] = swap_halves(slabs[j])[:, 0:64].astype(BF16)


def placed_back(parts):
    return pl.pallas_call(
        place_kernel,
        in_specs=[VMEM],
        out_specs=VMEM,
        out_shape=jax.ShapeDtypeStruct((2, 13, 13, 24, 64), BF16),
        compiler_params=params(SMALL),
        cost_estimate=cost(1e8, 3e6),
        name="placed_back",
    )(parts)


def fc_weight_kernel(place_ref, flat_0, flat_1, flat_2, flat_3, own_ref, other_ref, out_ref):
    core = place_ref[0]
    lead = first_half((576, 128))
    zero = jnp.zeros((576, 128), BF16)
    flats = [ref[h] for ref in (flat_0, flat_1, flat_2, flat_3) for h in range(2)]
    lefts = [
        jnp.concatenate([jnp.where(lead, flat, zero) for flat in flats], axis=1),
        jnp.concatenate([jnp.where(lead, zero, flat) for flat in flats], axis=1),
    ]
    for ref, parity in ((own_ref, core), (other_ref, 1 - core)):
        for half in range(2):
            right = jnp.concatenate(
                [ref[place_ref[1 + k], 128 * half : 128 * half + 128] for k in range(8)], axis=0
            )
            at = pl.ds(pl.multiple_of(parity * 256 + 128 * half, 128), 128)
            for t in range(2):
                out_ref[t, :, at] = nn_dot(lefts[t], right)


def fc_weight_grad_of(place, flats, own, other):
    return pl.pallas_call(
        fc_weight_kernel,
        in_specs=[SMEM] + [VMEM] * 6,
        out_specs=VMEM,
        out_shape=jax.ShapeDtypeStruct((2, 576, 512), F32),
        compiler_params=params(SMALL),
        cost_estimate=cost(3e9, 5e6),
        name="fc_weight_grad",
    )(place, *flats, own, other)


def row_of(column):
    size = column.shape[0]
    eye = lax.broadcasted_iota(jnp.int32, (size, size), 0) == lax.broadcasted_iota(jnp.int32, (size, size), 1)
    return jnp.sum(jnp.where(eye, column, 0.0), axis=0, keepdims=True)


def total_kernel(part_0, part_1, part_2, part_3, conv_ref, bias_ref, first_ref, fc_bias_ref, second_ref):
    total = (part_0[...].astype(F32) + part_1[...].astype(F32)) + (part_2[...].astype(F32) + part_3[...].astype(F32))
    conv_ref[...] = total[0:288]
    for t in range(2):
        fc_bias_ref[t : t + 1] = total[288 + t : 289 + t, 0:256]
        bias_ref[t : t + 1] = row_of(total[288:304, 260 + t : 261 + t])
    for u in range(2):
        for v in range(2):
            line = 290 + 2 * u + v
            second_ref[u, v : v + 1] = total[line : line + 1, 0:256]
            place = 256 + u if u == v else 258 + v
            first_ref[u, v : v + 1] = row_of(total[288:304, place : place + 1])


def summed(parts):
    return pl.pallas_call(
        total_kernel,
        in_specs=[VMEM] * 4,
        out_specs=[VMEM] * 5,
        out_shape=[
            jax.ShapeDtypeStruct((288, 384), F32),
            jax.ShapeDtypeStruct((2, 16), F32),
            jax.ShapeDtypeStruct((2, 2, 16), F32),
            jax.ShapeDtypeStruct((2, 256), F32),
            jax.ShapeDtypeStruct((2, 2, 256), F32),
        ],
        compiler_params=params(SMALL),
        cost_estimate=cost(1e7, 3e6),
        name="summed",
    )(*parts)


def mp_moves(z_step, y_step, core_step):
    return [
        ((z * 4 + y) * 2 + c, (((z + z_step) % 2) * 4 + (y + y_step) % 4) * 2 + (c + core_step) % 2)
        for z in range(2)
        for y in range(4)
        for c in range(2)
    ]


def dp_moves(x_step, z_step):
    return [(x * 2 + h, ((x + x_step) % 4) * 2 + (h + z_step) % 2) for x in range(4) for h in range(2)]


SAME_CORE = [[2 * k + c for k in range(8)] for c in range(2)]


def over_mp(array, z_step=0, y_step=0, core_step=0):
    return lax.ppermute(array, "mp", mp_moves(z_step, y_step, core_step))


def over_dp(array, x_step=0, z_step=0):
    return lax.ppermute(array, "dp", dp_moves(x_step, z_step))


def dealt(array, groups=None, axis="mp"):
    return lax.all_to_all(array, axis, 0, 0, tiled=True, axis_index_groups=groups)


def pick(array, index, axis):
    return lax.dynamic_index_in_dim(array, index, axis, keepdims=False)


def local(
    inputs,
    conv_weight,
    conv_bias,
    first_stitch,
    fc_weight,
    fc_bias,
    second_stitch,
    crop_counts,
    out_grad,
):
    x = jnp.transpose(inputs, (0, 2, 3, 1, 4))
    kernels = jnp.transpose(conv_weight, (0, 1, 2, 4, 3)).reshape(2, 144, 384)
    stitch_one = jnp.transpose(first_stitch, (1, 2, 0))
    mp_at, dp_at = lax.axis_index("mp"), lax.axis_index("dp")
    z_at, y_at, core = mp_at // 8, (mp_at // 2) % 4, mp_at % 2
    x_at, h_at = dp_at // 2, dp_at % 2
    core_arg = core.astype(jnp.int32).reshape(1)

    pair = jnp.stack([pick(kernels, core, 0), over_mp(pick(kernels, 1 - core, 0), core_step=1)])
    blocks = dealt(jnp.broadcast_to(pair[None], (8, 2, 144, 384)), SAME_CORE)
    slope, pooled, flat_t, own, other = front(
        core_arg, x, fc_weight, kernels.reshape(288, 384), conv_bias, stitch_one
    )
    own, blocks = lax.optimization_barrier((own, blocks))
    own = (own.astype(F32) + over_mp(other, core_step=1).astype(F32)).astype(BF16)
    parts = dealt(own, SAME_CORE)

    flat_z = over_dp(flat_t, z_step=1)
    parts, flat_z = lax.optimization_barrier((parts, flat_z))
    output, grad_copies, sums = hidden_layer(
        crop_counts,
        parts,
        fc_bias.T,
        jnp.transpose(second_stitch, (1, 2, 0)),
        jnp.transpose(out_grad, (1, 2, 0)),
    )
    grads_own = dealt(grad_copies, SAME_CORE)
    flat_pair = jnp.stack([flat_t, flat_z])
    flats = [flat_pair] + [over_dp(flat_pair, x_step=k) for k in range(1, 4)]
    grads_other = over_mp(grads_own, core_step=1)
    slice_own = dealt(grads_own, axis="dp")
    send, pre, stats = back_fc(core_arg, grads_own, grads_other, fc_weight, stitch_one, pooled, slope)
    send, slice_own, flats = lax.optimization_barrier((send, slice_own, flats))
    slice_other = over_mp(slice_own, core_step=1)
    pre_all = dealt(send)

    weight_part = weight_grad(x, pre, sums, stats)
    kernels_all = turned(core_arg, blocks)
    weight_z = over_dp(weight_part, z_step=1)
    pre_all, weight_part = lax.optimization_barrier((pre_all, weight_part))
    input_part = input_grad_part(pre_all, kernels_all)
    input_part, weight_z = lax.optimization_barrier((input_part, weight_z))
    weight_pair = (weight_part.astype(F32) + weight_z.astype(F32)).astype(BF16)
    part = dealt(input_part)

    conv_sum, conv_bias_grad, first_sum, fc_bias_sum, second_sum = summed(
        [weight_pair] + [over_dp(weight_pair, x_step=k) for k in range(1, 4)]
    )
    crops_place = jnp.stack(
        [core] + [(x_at + 4 - k) % 4 * 2 + (h_at + dh) % 2 for k in range(4) for dh in range(2)]
    ).astype(jnp.int32)
    fc_weight_grad = fc_weight_grad_of(crops_place, flats, slice_own, slice_other)
    input_grad = jnp.transpose(placed_back(part), (0, 4, 1, 2, 3))

    conv_weight_grad = jnp.transpose(conv_sum.reshape(2, 3, 3, 16, 384), (0, 1, 2, 4, 3))
    first_stitch_grad = jnp.transpose(first_sum, (2, 0, 1))
    fc_bias_grad = fc_bias_sum.T
    second_stitch_grad = jnp.transpose(second_sum, (2, 0, 1))
    return (
        jnp.transpose(output, (2, 0, 1)),
        input_grad,
        conv_weight_grad,
        conv_bias_grad,
        first_stitch_grad,
        fc_weight_grad,
        fc_bias_grad,
        second_stitch_grad,
    )


def solution(mesh):
    placed = (
        P(None, "dp", None, None, None),
        P(None, None, None, None, "mp"),
        P(None, "mp"),
        P("mp", None, None),
        P(None, "mp", None),
        P("mp", None),
        P("mp", None, None),
        P("dp"),
        P("mp", None, "dp"),
    )
    return jax.shard_map(
        local,
        mesh=mesh,
        in_specs=placed,
        out_specs=(
            P("mp", None, "dp"),
            P(None, "dp", None, None, "mp"),
            P(None, None, None, None, "mp"),
            P(None, "mp"),
            P("mp", None, None),
            P(None, "mp", "dp"),
            P("mp", None),
            P("mp", None, None),
        ),
        check_vma=False,
    )
```

```python
import jax
import jax.numpy as jnp
from jax import lax
from jax.experimental import pallas as pl
from jax.experimental.pallas import tpu as pltpu
from jax.sharding import PartitionSpec as P

F32 = jnp.float32
BF16 = jnp.bfloat16
LARGE, MEDIUM, SMALL = 56, 50, 16


def params(mib=LARGE):
    return pltpu.CompilerParams(vmem_limit_bytes=mib * 1024 * 1024)


def cost(flops, read):
    return pl.CostEstimate(flops=int(flops), bytes_accessed=int(read), transcendentals=0)


def nt_dot(left, right):
    return lax.dot_general(left, right, (((1,), (1,)), ((), ())), preferred_element_type=F32)


def nn_dot(left, right):
    return lax.dot_general(left, right, (((1,), (0,)), ((), ())), preferred_element_type=F32)


def first_half(shape):
    return lax.broadcasted_iota(jnp.int32, shape, len(shape) - 1) < 64


def swap_halves(value):
    return pltpu.roll(value, 64, value.ndim - 1)


def gelu_parts(x):
    root, cubic = 0.7978845608028654, 0.044715
    square = x * x
    tanh = jnp.tanh(root * x * (1.0 + cubic * square))
    half = 0.5 + 0.5 * tanh
    slope = half + 0.5 * x * (1.0 - tanh * tanh) * (root * (1.0 + 3.0 * cubic * square))
    return x * half, slope


def spread(slabs):
    lane = lax.broadcasted_iota(jnp.int32, slabs[0].shape, 1)
    for bit in range(4):
        odd = (lane & (8 << bit)) != 0
        slabs = [jnp.where(odd, slabs[(k + (1 << bit)) % 16], slabs[k]) for k in range(16)]
    return slabs


def exchange(slabs):
    slabs = spread(slabs)
    slabs = [slabs[0]] + [pltpu.roll(slabs[k], 8 * k, 1) for k in range(1, 16)]
    slabs = spread(slabs)
    return [slabs[-k % 16] for k in range(16)]


def column(row):
    size = row.shape[1]
    eye = lax.broadcasted_iota(jnp.int32, (size, size), 0) == lax.broadcasted_iota(jnp.int32, (size, size), 1)
    return jnp.sum(jnp.where(eye, row, 0.0), axis=1, keepdims=True)


def by_tower(first, second):
    lead = first_half((16, 128))
    return jnp.where(lead, column(first), column(second))


def stitch_slabs(stitch_ref):
    part = [[stitch_ref[u, v : v + 1] for v in range(2)] for u in range(2)]
    own = by_tower(part[0][0], part[1][1])
    into = by_tower(part[0][1], part[1][0])
    back = by_tower(part[1][0], part[0][1])
    return own, into, back


def slab_order(fc_axis):
    fc_row = lax.broadcasted_iota(jnp.int32, (576, 576), fc_axis)
    slab_row = lax.broadcasted_iota(jnp.int32, (576, 576), 1 - fc_axis)
    return (fc_row == 36 * (slab_row & 15) + (slab_row >> 4)).astype(F32).astype(BF16)


def front_kernel(
    core_ref, x_ref, w_ref, kernel_ref, bias_ref, stitch_ref,
    slope_ref, pooled_ref, flat_t_ref, own_ref, other_ref,
    xs, ws, acc, ready, pool, slopes, pooled_out, flat_t_out, parts, x_sem, w_sem, slope_sem, out_sem,
):
    def x_copy(i):
        return pltpu.make_async_copy(x_ref.at[:, i], xs.at[:, i], x_sem.at[i])

    def w_copy(t):
        return pltpu.make_async_copy(w_ref.at[t], ws.at[t], w_sem.at[t])

    def slope_copy(i):
        return pltpu.make_async_copy(slopes.at[i], slope_ref.at[i], slope_sem.at[i])

    for i in range(13):
        x_copy(i).start()
    for t in range(2):
        w_copy(t).start()
    acc[...] = jnp.zeros_like(acc)
    ready[...] = jnp.zeros_like(ready)
    pool[...] = jnp.zeros_like(pool)
    lead = first_half((16, 128))
    bias = by_tower(bias_ref[0:1], bias_ref[1:2])
    own, into, _ = stitch_slabs(stitch_ref)

    def gather(row):
        line = jnp.maximum(row + 1, 0)
        for t in range(2):
            right = pltpu.roll(acc[t, 0, line], 64, 1)
            left = pltpu.roll(acc[t, 2, line], 832, 1)
            ready[t] = acc[t, 1, line] + right + left

    def finish(row):
        acts = []
        for j in range(13):
            lanes = slice(j // 2 * 128, j // 2 * 128 + 128)
            zero, one = ready[0, :, lanes], ready[1, :, lanes]
            if j % 2 == 0:
                pre_act = jnp.where(lead, zero, swap_halves(one))
            else:
                pre_act = jnp.where(lead, swap_halves(zero), one)
            act, slope = gelu_parts(pre_act + bias)
            slopes[jnp.maximum(row, 0), j] = slope.astype(BF16)
            acts.append(act)
        even = row % 2 == 0
        for q in range(6):
            total = acts[2 * q] + acts[2 * q + 1] + acts[2 * q + 2]
            pool[jnp.maximum(row + 2, 0) // 2, q] += total
            pool[jnp.maximum(row, 0) // 2, q] += jnp.where(even, total, 0.0)

    def line(i, carry):
        x_copy(i).wait()
        finish(i - 3)
        gather(i - 2)
        for t in range(2):
            weights = kernel_ref[144 * t : 144 * t + 144]
            for start in range(0, 13, 4):
                width = min(4, 13 - start)
                rows = xs[t, i, start : start + width].reshape(64 * width, 384)
                product = nt_dot(weights, rows)
                for a in range(3):
                    for b in range(3):
                        top = 16 * (3 * a + b)
                        acc[t, b, i + 2 - a, :, 64 * start : 64 * (start + width)] += product[top : top + 16]
        return carry

    def last(i, carry):
        finish(i - 3)
        gather(jnp.minimum(i - 2, 12))
        return carry

    lax.fori_loop(0, 13, line, 0)
    lax.fori_loop(13, 16, last, 0)
    for i in range(13):
        slope_copy(i).start()
    pooled = pool[1:7].reshape(36, 16, 128) * (1.0 / 9.0)
    pooled_out[...] = pooled
    pooled_copy = pltpu.make_async_copy(pooled_out, pooled_ref, out_sem.at[0])
    pooled_copy.start()
    mixed = own[None] * pooled + into[None] * swap_halves(pooled)
    flat_t = nn_dot(slab_order(0), mixed.reshape(576, 128).astype(BF16))
    flat_t_out[...] = flat_t.astype(BF16)
    flat_copy = pltpu.make_async_copy(flat_t_out, flat_t_ref, out_sem.at[1])
    flat_copy.start()
    flat = flat_t.T.astype(BF16)
    core = core_ref[0]
    copies_out = [pooled_copy, flat_copy]
    for t in range(2):
        w_copy(t).wait()
    for k, (ref, parity) in enumerate(((other_ref, 1 - core), (own_ref, core))):
        for q in range(8):
            at = pl.ds(pl.multiple_of((2 * q + parity) * 256, 256), 256)
            for t in range(2):
                parts[k, q, 64 * t : 64 * t + 64] = nn_dot(flat[64 * t : 64 * t + 64], ws[t, :, at]).astype(BF16)
            if q % 4 == 3:
                some = pl.ds(q - 3, 4)
                copy = pltpu.make_async_copy(parts.at[k, some], ref.at[some], out_sem.at[2 + 2 * k + q // 4])
                copy.start()
                copies_out.append(copy)
    for i in range(13):
        slope_copy(i).wait()
    for copy in copies_out:
        copy.wait()


VMEM = pl.BlockSpec(memory_space=pltpu.VMEM)
SMEM = pl.BlockSpec(memory_space=pltpu.SMEM)
ANY = pl.BlockSpec(memory_space=pl.ANY)


def front(core, x, w, kernels, bias, stitch):
    return pl.pallas_call(
        front_kernel,
        in_specs=[SMEM, ANY, ANY, VMEM, VMEM, VMEM],
        out_specs=[ANY] * 5,
        out_shape=[
            jax.ShapeDtypeStruct((13, 13, 16, 128), BF16),
            jax.ShapeDtypeStruct((36, 16, 128), F32),
            jax.ShapeDtypeStruct((576, 128), BF16),
            jax.ShapeDtypeStruct((8, 128, 256), BF16),
            jax.ShapeDtypeStruct((8, 128, 256), BF16),
        ],
        scratch_shapes=[
            pltpu.VMEM((2, 13, 13, 64, 384), BF16),
            pltpu.VMEM((2, 576, 4096), BF16),
            pltpu.VMEM((2, 3, 15, 16, 896), F32),
            pltpu.VMEM((2, 16, 896), F32),
            pltpu.VMEM((8, 6, 16, 128), F32),
            pltpu.VMEM((13, 13, 16, 128), BF16),
            pltpu.VMEM((36, 16, 128), F32),
            pltpu.VMEM((576, 128), BF16),
            pltpu.VMEM((2, 8, 128, 256), BF16),
            pltpu.SemaphoreType.DMA((13,)),
            pltpu.SemaphoreType.DMA((2,)),
            pltpu.SemaphoreType.DMA((13,)),
            pltpu.SemaphoreType.DMA((6,)),
        ],
        compiler_params=params(),
        cost_estimate=cost(10e9, 30e6),
        name="front",
    )(core, x, w, kernels, bias, stitch)


def pair_kernel(first_ref, second_ref, out_ref):
    out_ref[...] = (first_ref[...].astype(F32) + second_ref[...].astype(F32)).astype(BF16)


def pair_sum(first, second):
    return pl.pallas_call(
        pair_kernel,
        in_specs=[VMEM, VMEM],
        out_specs=VMEM,
        out_shape=jax.ShapeDtypeStruct(first.shape, BF16),
        compiler_params=params(SMALL),
        cost_estimate=cost(1e6, 2e6),
        name="pair_sum",
    )(first, second)


def fan_kernel(core_ref, near_ref, far_ref, out_ref, held, in_sem, out_sem):
    core = core_ref[0]
    for p, ref in enumerate((near_ref, far_ref)):
        pltpu.make_async_copy(ref.at[core], held.at[p], in_sem.at[p]).start()
    for p, ref in enumerate((near_ref, far_ref)):
        pltpu.make_async_copy(ref.at[core], held.at[p], in_sem.at[p]).wait()
    copies = [pltpu.make_async_copy(held, out_ref.at[k], out_sem.at[k]) for k in range(8)]
    for copy in copies:
        copy.start()
    for copy in copies:
        copy.wait()


def fanned(core, near, far):
    return pl.pallas_call(
        fan_kernel,
        in_specs=[SMEM, ANY, ANY],
        out_specs=ANY,
        out_shape=jax.ShapeDtypeStruct((8, 2, 144, 384), BF16),
        scratch_shapes=[
            pltpu.VMEM((2, 144, 384), BF16),
            pltpu.SemaphoreType.DMA((2,)),
            pltpu.SemaphoreType.DMA((8,)),
        ],
        compiler_params=params(SMALL),
        cost_estimate=cost(1e6, 4e6),
        name="fanned",
    )(core, near, far)


def hidden_kernel(counts_ref, parts_ref, bias_ref, stitch_ref, cot_ref, out_ref, grad_ref, sums_ref):
    live = counts_ref[0]
    for k in range(1, 8):
        live += counts_ref[k]
    mask = (lax.broadcasted_iota(jnp.int32, (64, 256), 0) < live).astype(F32)
    total = parts_ref[0].astype(F32)
    for k in range(1, 8):
        total += parts_ref[k].astype(F32)
    hidden, slope = [], []
    for t in range(2):
        act, der = gelu_parts(total[64 * t : 64 * t + 64] + bias_ref[t][None])
        hidden.append(act)
        slope.append(der)
    cots = [cot_ref[u].astype(F32) * mask for u in range(2)]
    stitch = [[stitch_ref[u, v][None] for v in range(2)] for u in range(2)]
    sums = []
    for u in range(2):
        out_ref[u] = (mask * (stitch[u][0] * hidden[0] + stitch[u][1] * hidden[1])).astype(BF16)
    for v in range(2):
        grad = (stitch[0][v] * cots[0] + stitch[1][v] * cots[1]) * slope[v]
        grad = grad.astype(BF16)
        for k in range(8):
            for half in range(2):
                top = 128 * half + 64 * v
                grad_ref[k, top : top + 64] = grad[:, 128 * half : 128 * half + 128]
        sums.append(jnp.sum(grad.astype(F32), axis=0, keepdims=True))
    for u in range(2):
        for v in range(2):
            sums.append(jnp.sum(cots[u] * hidden[v], axis=0, keepdims=True))
    sums_ref[...] = jnp.concatenate(sums + [jnp.zeros((2, 256), F32)], axis=0)


def hidden_layer(counts, parts, bias, stitch, cot):
    vmem = pl.BlockSpec(memory_space=pltpu.VMEM)
    return pl.pallas_call(
        hidden_kernel,
        in_specs=[pl.BlockSpec(memory_space=pltpu.SMEM), vmem, vmem, vmem, vmem],
        out_specs=[vmem, vmem, vmem],
        out_shape=[
            jax.ShapeDtypeStruct((2, 64, 256), BF16),
            jax.ShapeDtypeStruct((8, 256, 128), BF16),
            jax.ShapeDtypeStruct((8, 256), F32),
        ],
        compiler_params=params(SMALL),
        cost_estimate=cost(1e7, 3e6),
        name="hidden_layer",
    )(counts, parts, bias, stitch, cot)


def back_kernel(
    core_ref, own_ref, other_ref, w_ref, stitch_ref, pooled_ref, slope_ref,
    send_ref, pre_ref, stats_ref,
    ws, pooled, slopes, sends, w_sem, in_sem, send_sem,
):
    def w_copy(k):
        at = pl.ds(1024 * k, 1024)
        return pltpu.make_async_copy(w_ref.at[:, :, at], ws.at[:, :, at], w_sem.at[k])

    later_in = [
        pltpu.make_async_copy(pooled_ref, pooled, in_sem.at[0]),
        pltpu.make_async_copy(slope_ref, slopes, in_sem.at[1]),
    ]
    for k in range(4):
        w_copy(k).start()
    for copy in later_in:
        copy.start()
    first = core_ref[0] == 0
    perm = slab_order(1)
    own_slab, _, back_slab = stitch_slabs(stitch_ref)
    totals = [jnp.zeros((576, 128), F32)] * 2
    for k in range(4):
        w_copy(k).wait()
        blocks = []
        for q in (2 * k, 2 * k + 1):
            own, other = (jnp.concatenate([ref[q, 0:128], ref[q, 128:256]], axis=1) for ref in (own_ref, other_ref))
            blocks += [jnp.where(first, own, other), jnp.where(first, other, own)]
        rows = jnp.concatenate(blocks, axis=1)
        for t in range(2):
            totals[t] = totals[t] + nt_dot(ws[t, :, 1024 * k : 1024 * k + 1024], rows)
    flat_grad = jnp.where(first_half((576, 128)), totals[0], totals[1])
    high = flat_grad.astype(BF16)
    low = (flat_grad - high.astype(F32)).astype(BF16)
    mixed_grad = (nn_dot(perm, high) + nn_dot(perm, low)).reshape(36, 16, 128)
    swapped = swap_halves(mixed_grad)
    pooled_grad = own_slab[None] * mixed_grad + back_slab[None] * swapped
    pooled_grad = (pooled_grad * (1.0 / 9.0)).reshape(6, 6, 16, 128)
    for copy in later_in:
        copy.wait()
    lead = first_half((16, 128))
    bias_sum = jnp.zeros((16, 128), F32)
    zero = jnp.zeros((16, 128), F32)
    widened = []
    for p in range(6):
        line = []
        for j in range(13):
            terms = [pooled_grad[p, q] for q in range(6) if 2 * q <= j <= 2 * q + 2]
            line.append(terms[0] if len(terms) == 1 else terms[0] + terms[1])
        widened.append(line)
    copies_out = []
    for i in range(13):
        windows = [p for p in range(6) if 2 * p <= i <= 2 * p + 2]
        slabs = []
        for j in range(13):
            value = widened[windows[0]][j]
            if len(windows) == 2:
                value = value + widened[windows[1]][j]
            value = (value * slopes[i, j].astype(F32)).astype(BF16)
            pre_ref[i, j] = value
            value = value.astype(F32)
            bias_sum = bias_sum + value
            slabs.append(value)
        slabs = exchange(slabs + [zero] * 3)
        at = pl.ds(128 * i, 128)
        for m in range(16):
            block = (m % 2) * 8 + m // 2
            sends[m, :, 128 * i : 128 * i + 128] = slabs[block].astype(BF16)
        copies_out.append(pltpu.make_async_copy(sends.at[:, :, at], send_ref.at[:, :, at], send_sem.at[i]))
        copies_out[-1].start()
    pooled_in = pooled[...]
    own = jnp.sum(mixed_grad * pooled_in, axis=0)
    cross = jnp.sum(swapped * pooled_in, axis=0)
    lane = lax.broadcasted_iota(jnp.int32, (16, 128), 1)
    stats = jnp.zeros((16, 128), F32)
    for k, value in enumerate((own, cross, bias_sum)):
        for t in range(2):
            half = jnp.sum(jnp.where(lead == (t == 0), value, 0.0), axis=1, keepdims=True)
            stats = jnp.where(lane == 2 * k + t, half, stats)
    stats_ref[...] = stats
    for copy in copies_out:
        copy.wait()


def back_fc(core, own, other, w, stitch, pooled, slope):
    return pl.pallas_call(
        back_kernel,
        in_specs=[SMEM, VMEM, VMEM, ANY, VMEM, ANY, ANY],
        out_specs=[ANY, VMEM, VMEM],
        out_shape=[
            jax.ShapeDtypeStruct((16, 16, 1664), BF16),
            jax.ShapeDtypeStruct((13, 13, 16, 128), BF16),
            jax.ShapeDtypeStruct((16, 128), F32),
        ],
        scratch_shapes=[
            pltpu.VMEM((2, 576, 4096), BF16),
            pltpu.VMEM((36, 16, 128), F32),
            pltpu.VMEM((13, 13, 16, 128), BF16),
            pltpu.VMEM((16, 16, 1664), BF16),
            pltpu.SemaphoreType.DMA((4,)),
            pltpu.SemaphoreType.DMA((2,)),
            pltpu.SemaphoreType.DMA((13,)),
        ],
        compiler_params=params(),
        cost_estimate=cost(1e8, 1e6),
        name="back_fc",
    )(core, own, other, w, stitch, pooled, slope)


def weight_kernel(x_ref, pre_ref, sums_ref, stats_ref, out_ref, xs, lines, acc, x_sem):
    def x_copy(i):
        return pltpu.make_async_copy(x_ref.at[:, i], xs.at[:, i], x_sem.at[i])

    for i in range(13):
        x_copy(i).start()
    lines[...] = jnp.zeros_like(lines)
    acc[...] = jnp.zeros_like(acc)
    lead = first_half((16, 128))

    def merge(i, carry):
        zero = jnp.zeros((16, 128), F32)
        slabs = [pre_ref[i, j].astype(F32) for j in range(13)]
        turned = [swap_halves(slab) for slab in slabs]
        slabs = [zero] + slabs + [zero] * 2
        turned = [zero] + turned + [zero] * 2
        for first in range(-1, 14):
            left, right = first + 1, first + 2
            pair = (
                jnp.where(lead, slabs[left], turned[right]).astype(BF16),
                jnp.where(lead, turned[left], slabs[right]).astype(BF16),
            )
            for b in range(3):
                place = first + b - 1
                if place % 2 == 0 and 0 <= place <= 12:
                    for t in range(2):
                        lines[t, b, i + 1, :, 64 * place : 64 * place + 128] = pair[t]
        return carry

    lax.fori_loop(0, 13, merge, 0)

    def line(i, carry):
        x_copy(i).wait()
        for t in range(2):
            left = jnp.concatenate([lines[t, b, i + 2 - a] for a in range(3) for b in range(3)], axis=0)
            right = jnp.concatenate([xs[t, i].reshape(832, 384), jnp.zeros((64, 384), BF16)], axis=0)
            acc[144 * t : 144 * t + 144] += nn_dot(left, right)
        return carry

    lax.fori_loop(0, 13, line, 0)
    out_ref[0:288] = acc[...].astype(BF16)
    small = jnp.concatenate([sums_ref[...], jnp.zeros((8, 256), F32)], axis=0)
    out_ref[288:304] = jnp.concatenate([small, stats_ref[...]], axis=1).astype(BF16)


def weight_grad(x, pre, sums, stats):
    return pl.pallas_call(
        weight_kernel,
        in_specs=[ANY, VMEM, VMEM, VMEM],
        out_specs=VMEM,
        out_shape=jax.ShapeDtypeStruct((304, 384), BF16),
        scratch_shapes=[
            pltpu.VMEM((2, 13, 13, 64, 384), BF16),
            pltpu.VMEM((2, 3, 15, 16, 896), BF16),
            pltpu.VMEM((288, 384), F32),
            pltpu.SemaphoreType.DMA((13,)),
        ],
        compiler_params=params(MEDIUM),
        cost_estimate=cost(10e9, 20e6),
        name="weight_grad",
    )(x, pre, sums, stats)


def turn_kernel(core_ref, blocks_ref, out_ref, rows):
    core = core_ref[0]
    for k in range(8):
        for p, parity in ((0, core), (1, 1 - core)):
            at = pl.ds(pl.multiple_of(16 * (2 * k + parity), 16), 16)
            for tap in range(9):
                rows[tap, at] = blocks_ref[k, p, 16 * tap : 16 * tap + 16]
    for tap in range(9):
        out_ref[:, 256 * tap : 256 * tap + 256] = rows[tap].T


def turned(core, blocks):
    return pl.pallas_call(
        turn_kernel,
        in_specs=[SMEM, VMEM],
        out_specs=VMEM,
        out_shape=jax.ShapeDtypeStruct((384, 2304), BF16),
        scratch_shapes=[pltpu.VMEM((9, 256, 384), BF16)],
        compiler_params=params(SMALL),
        cost_estimate=cost(1e9, 4e6),
        name="turned_kernels",
    )(core, blocks)


def input_kernel(g_ref, w_ref, out_ref, taps):
    g = g_ref[...].reshape(256, 1664).astype(F32)
    zero = jnp.zeros((256, 128), BF16)
    for b in range(3):
        taps[b, :, 0:128] = zero
        taps[b, :, 1792:1920] = zero
        for i in range(13):
            row = g[:, 128 * i : 128 * i + 128]
            if b == 0:
                row = pltpu.roll(row, 120, 1)
            if b == 2:
                row = pltpu.roll(row, 8, 1)
            taps[b, :, 128 * i + 128 : 128 * i + 256] = row.astype(BF16)
    weights = w_ref[...]
    for start in range(0, 13, 2):
        width = 128 * min(2, 13 - start)
        right = jnp.concatenate(
            [
                taps[b, :, 128 * (start + 2 - a) : 128 * (start + 2 - a) + width]
                for a in range(3)
                for b in range(3)
            ],
            axis=0,
        )
        product = nn_dot(weights, right)
        for m in range(16):
            out_ref[m, :, 128 * start : 128 * start + width] = product[24 * m : 24 * m + 24].astype(BF16)


def input_grad_part(g, w):
    return pl.pallas_call(
        input_kernel,
        in_specs=[VMEM, VMEM],
        out_specs=VMEM,
        out_shape=jax.ShapeDtypeStruct((16, 24, 1664), BF16),
        scratch_shapes=[pltpu.VMEM((3, 256, 1920), BF16)],
        compiler_params=params(SMALL),
        cost_estimate=cost(4e9, 4e6),
        name="input_grad",
    )(g, w)


def place_kernel(part_ref, out_ref, rows, sem):
    copies = [pltpu.make_async_copy(rows.at[:, i], out_ref.at[:, i], sem.at[i]) for i in range(13)]
    for i in range(13):
        lanes = slice(128 * i, 128 * i + 128)
        slabs = [part_ref[2 * (block % 8) + block // 8, :, lanes].astype(F32) for block in range(16)]
        slabs = exchange(slabs)
        for j in range(13):
            rows[0, i, j] = slabs[j][:, 0:64].astype(BF16)
            rows[1, i, j] = swap_halves(slabs[j])[:, 0:64].astype(BF16)
        copies[i].start()
    for copy in copies:
        copy.wait()


def placed_back(parts):
    return pl.pallas_call(
        place_kernel,
        in_specs=[VMEM],
        out_specs=ANY,
        out_shape=jax.ShapeDtypeStruct((2, 13, 13, 24, 64), BF16),
        scratch_shapes=[pltpu.VMEM((2, 13, 13, 24, 64), BF16), pltpu.SemaphoreType.DMA((13,))],
        compiler_params=params(SMALL),
        cost_estimate=cost(1e8, 3e6),
        name="placed_back",
    )(parts)


def fc_weight_kernel(place_ref, flat_0, flat_1, flat_3, near_2, far_2, own_ref, other_ref, out_ref):
    core = place_ref[0]
    lead = first_half((576, 128))
    zero = jnp.zeros((576, 128), BF16)
    flats = [ref[h] for ref in (flat_0, flat_1, flat_3) for h in range(2)] + [near_2[...], far_2[...]]
    lefts = [
        jnp.concatenate([jnp.where(lead, flat, zero) for flat in flats], axis=1),
        jnp.concatenate([jnp.where(lead, zero, flat) for flat in flats], axis=1),
    ]
    for ref, parity in ((own_ref, core), (other_ref, 1 - core)):
        for half in range(2):
            right = jnp.concatenate(
                [ref[place_ref[1 + k], 128 * half : 128 * half + 128] for k in range(8)], axis=0
            )
            at = pl.ds(pl.multiple_of(parity * 256 + 128 * half, 128), 128)
            for t in range(2):
                out_ref[t, :, at] = nn_dot(lefts[t], right)


def fc_weight_grad_of(place, flats, own, other):
    return pl.pallas_call(
        fc_weight_kernel,
        in_specs=[SMEM] + [VMEM] * 7,
        out_specs=VMEM,
        out_shape=jax.ShapeDtypeStruct((2, 576, 512), F32),
        compiler_params=params(SMALL),
        cost_estimate=cost(3e9, 5e6),
        name="fc_weight_grad",
    )(place, *flats, own, other)


def row_of(column):
    size = column.shape[0]
    eye = lax.broadcasted_iota(jnp.int32, (size, size), 0) == lax.broadcasted_iota(jnp.int32, (size, size), 1)
    return jnp.sum(jnp.where(eye, column, 0.0), axis=0, keepdims=True)


def total_kernel(part_0, part_1, part_2, part_3, conv_ref, bias_ref, first_ref, fc_bias_ref, second_ref):
    total = (part_0[...].astype(F32) + part_1[...].astype(F32)) + (part_2[...].astype(F32) + part_3[...].astype(F32))
    conv_ref[...] = total[0:288]
    for t in range(2):
        fc_bias_ref[t : t + 1] = total[288 + t : 289 + t, 0:256]
        bias_ref[t : t + 1] = row_of(total[288:304, 260 + t : 261 + t])
    for u in range(2):
        for v in range(2):
            line = 290 + 2 * u + v
            second_ref[u, v : v + 1] = total[line : line + 1, 0:256]
            place = 256 + u if u == v else 258 + v
            first_ref[u, v : v + 1] = row_of(total[288:304, place : place + 1])


def summed(parts):
    return pl.pallas_call(
        total_kernel,
        in_specs=[VMEM] * 4,
        out_specs=[VMEM] * 5,
        out_shape=[
            jax.ShapeDtypeStruct((288, 384), F32),
            jax.ShapeDtypeStruct((2, 16), F32),
            jax.ShapeDtypeStruct((2, 2, 16), F32),
            jax.ShapeDtypeStruct((2, 256), F32),
            jax.ShapeDtypeStruct((2, 2, 256), F32),
        ],
        compiler_params=params(SMALL),
        cost_estimate=cost(1e7, 3e6),
        name="summed",
    )(*parts)


def mp_moves(z_step, y_step, core_step):
    return [
        ((z * 4 + y) * 2 + c, (((z + z_step) % 2) * 4 + (y + y_step) % 4) * 2 + (c + core_step) % 2)
        for z in range(2)
        for y in range(4)
        for c in range(2)
    ]


def dp_moves(x_step, z_step):
    return [(x * 2 + h, ((x + x_step) % 4) * 2 + (h + z_step) % 2) for x in range(4) for h in range(2)]


SAME_CORE = [[2 * k + c for k in range(8)] for c in range(2)]


def over_mp(array, z_step=0, y_step=0, core_step=0):
    return lax.ppermute(array, "mp", mp_moves(z_step, y_step, core_step))


def over_dp(array, x_step=0, z_step=0):
    return lax.ppermute(array, "dp", dp_moves(x_step, z_step))


def dealt(array, groups=None, axis="mp"):
    return lax.all_to_all(array, axis, 0, 0, tiled=True, axis_index_groups=groups)


def pick(array, index, axis):
    return lax.dynamic_index_in_dim(array, index, axis, keepdims=False)


def local(
    inputs,
    conv_weight,
    conv_bias,
    first_stitch,
    fc_weight,
    fc_bias,
    second_stitch,
    crop_counts,
    out_grad,
):
    x = jnp.transpose(inputs, (0, 2, 3, 1, 4))
    kernels = jnp.transpose(conv_weight, (0, 1, 2, 4, 3)).reshape(2, 144, 384)
    stitch_one = jnp.transpose(first_stitch, (1, 2, 0))
    mp_at, dp_at = lax.axis_index("mp"), lax.axis_index("dp")
    z_at, y_at, core = mp_at // 8, (mp_at // 2) % 4, mp_at % 2
    x_at, h_at = dp_at // 2, dp_at % 2
    core_arg = core.astype(jnp.int32).reshape(1)

    kernels_c = over_mp(kernels, core_step=1)
    blocks = dealt(fanned(core_arg, kernels, kernels_c), SAME_CORE)
    slope, pooled, flat_t, own, other = front(
        core_arg, x, fc_weight, kernels.reshape(288, 384), conv_bias, stitch_one
    )
    flat_z, flat_2 = over_dp(flat_t, z_step=1), over_dp(flat_t, x_step=2)
    own, blocks = lax.optimization_barrier((own, blocks))
    own = pair_sum(own, over_mp(other, core_step=1))
    own, flat_z, flat_2 = lax.optimization_barrier((own, flat_z, flat_2))
    parts = dealt(own, SAME_CORE)

    flat_pair = jnp.stack([flat_t, flat_z])
    flat_1, flat_3 = over_dp(flat_pair, x_step=1), over_dp(flat_pair, x_step=3)
    output, grad_copies, sums = hidden_layer(
        crop_counts,
        parts,
        fc_bias.T,
        jnp.transpose(second_stitch, (1, 2, 0)),
        jnp.transpose(out_grad, (1, 2, 0)),
    )
    grad_copies, flat_1, flat_3 = lax.optimization_barrier((grad_copies, flat_1, flat_3))
    grads_own = dealt(grad_copies, SAME_CORE)
    flats = [flat_pair, flat_1, flat_3, flat_2, over_dp(flat_z, x_step=2)]
    kernels_all = turned(core_arg, blocks)
    grads_own, flats, kernels_all = lax.optimization_barrier((grads_own, flats, kernels_all))
    grads_other = over_mp(grads_own, core_step=1)
    slice_own = dealt(grads_own, axis="dp")
    send, pre, stats = back_fc(core_arg, grads_own, grads_other, fc_weight, stitch_one, pooled, slope)
    send, slice_own = lax.optimization_barrier((send, slice_own))
    slice_other = over_mp(slice_own, core_step=1)
    pre_all = dealt(send)

    weight_part = weight_grad(x, pre, sums, stats)
    weight_z = over_dp(weight_part, z_step=1)
    pre_all, weight_part = lax.optimization_barrier((pre_all, weight_part))
    input_part = input_grad_part(pre_all, kernels_all)
    input_part, weight_z = lax.optimization_barrier((input_part, weight_z))
    part = dealt(input_part)

    weight_pair = pair_sum(weight_part, weight_z)
    conv_sum, conv_bias_grad, first_sum, fc_bias_sum, second_sum = summed(
        [weight_pair] + [over_dp(weight_pair, x_step=k) for k in range(1, 4)]
    )
    crops_place = jnp.stack(
        [core] + [(x_at + 4 - k) % 4 * 2 + (h_at + dh) % 2 for k in (0, 1, 3, 2) for dh in range(2)]
    ).astype(jnp.int32)
    fc_weight_grad = fc_weight_grad_of(crops_place, flats, slice_own, slice_other)
    input_grad = jnp.transpose(placed_back(part), (0, 4, 1, 2, 3))

    conv_weight_grad = jnp.transpose(conv_sum.reshape(2, 3, 3, 16, 384), (0, 1, 2, 4, 3))
    first_stitch_grad = jnp.transpose(first_sum, (2, 0, 1))
    fc_bias_grad = fc_bias_sum.T
    second_stitch_grad = jnp.transpose(second_sum, (2, 0, 1))
    return (
        jnp.transpose(output, (2, 0, 1)),
        input_grad,
        conv_weight_grad,
        conv_bias_grad,
        first_stitch_grad,
        fc_weight_grad,
        fc_bias_grad,
        second_stitch_grad,
    )


def solution(mesh):
    placed = (
        P(None, "dp", None, None, None),
        P(None, None, None, None, "mp"),
        P(None, "mp"),
        P("mp", None, None),
        P(None, "mp", None),
        P("mp", None),
        P("mp", None, None),
        P("dp"),
        P("mp", None, "dp"),
    )
    return jax.shard_map(
        local,
        mesh=mesh,
        in_specs=placed,
        out_specs=(
            P("mp", None, "dp"),
            P(None, "dp", None, None, "mp"),
            P(None, None, None, None, "mp"),
            P(None, "mp"),
            P("mp", None, None),
            P(None, "mp", "dp"),
            P("mp", None),
            P("mp", None, None),
        ),
        check_vma=False,
    )
```

```python
import jax
import jax.numpy as jnp
from jax import lax
from jax.experimental import pallas as pl
from jax.experimental.pallas import tpu as pltpu
from jax.sharding import PartitionSpec as P

F32 = jnp.float32
BF16 = jnp.bfloat16
LARGE, MEDIUM, SMALL = 56, 50, 16


def params(mib=LARGE):
    return pltpu.CompilerParams(vmem_limit_bytes=mib * 1024 * 1024)


def cost(flops, read):
    return pl.CostEstimate(flops=int(flops), bytes_accessed=int(read), transcendentals=0)


def nt_dot(left, right):
    return lax.dot_general(left, right, (((1,), (1,)), ((), ())), preferred_element_type=F32)


def nn_dot(left, right):
    return lax.dot_general(left, right, (((1,), (0,)), ((), ())), preferred_element_type=F32)


def first_half(shape):
    return lax.broadcasted_iota(jnp.int32, shape, len(shape) - 1) < 64


def swap_halves(value):
    return pltpu.roll(value, 64, value.ndim - 1)


def gelu_parts(x):
    root, cubic = 0.7978845608028654, 0.044715
    square = x * x
    tanh = jnp.tanh(root * x * (1.0 + cubic * square))
    half = 0.5 + 0.5 * tanh
    slope = half + 0.5 * x * (1.0 - tanh * tanh) * (root * (1.0 + 3.0 * cubic * square))
    return x * half, slope


def spread(slabs):
    lane = lax.broadcasted_iota(jnp.int32, slabs[0].shape, 1)
    for bit in range(4):
        odd = (lane & (8 << bit)) != 0
        slabs = [jnp.where(odd, slabs[(k + (1 << bit)) % 16], slabs[k]) for k in range(16)]
    return slabs


def exchange(slabs):
    slabs = spread(slabs)
    slabs = [slabs[0]] + [pltpu.roll(slabs[k], 8 * k, 1) for k in range(1, 16)]
    slabs = spread(slabs)
    return [slabs[-k % 16] for k in range(16)]


def column(row):
    size = row.shape[1]
    eye = lax.broadcasted_iota(jnp.int32, (size, size), 0) == lax.broadcasted_iota(jnp.int32, (size, size), 1)
    return jnp.sum(jnp.where(eye, row, 0.0), axis=1, keepdims=True)


def by_tower(first, second):
    lead = first_half((16, 128))
    return jnp.where(lead, column(first), column(second))


def stitch_slabs(stitch_ref):
    part = [[stitch_ref[u, v : v + 1] for v in range(2)] for u in range(2)]
    own = by_tower(part[0][0], part[1][1])
    into = by_tower(part[0][1], part[1][0])
    back = by_tower(part[1][0], part[0][1])
    return own, into, back


def slab_order(fc_axis):
    fc_row = lax.broadcasted_iota(jnp.int32, (576, 576), fc_axis)
    slab_row = lax.broadcasted_iota(jnp.int32, (576, 576), 1 - fc_axis)
    return (fc_row == 36 * (slab_row & 15) + (slab_row >> 4)).astype(F32).astype(BF16)


def front_kernel(
    core_ref, x_ref, w_ref, kernel_ref, bias_ref, stitch_ref,
    slope_ref, pooled_ref, flat_t_ref, own_ref, other_ref,
    xs, ws, acc, ready, pool, slopes, pooled_out, flat_t_out, x_sem, w_sem, slope_sem, out_sem,
):
    def x_copy(i):
        return pltpu.make_async_copy(x_ref.at[:, i], xs.at[:, i], x_sem.at[i])

    def w_copy(t):
        return pltpu.make_async_copy(w_ref.at[t], ws.at[t], w_sem.at[t])

    def slope_copy(i):
        return pltpu.make_async_copy(slopes.at[i], slope_ref.at[i], slope_sem.at[i])

    for i in range(13):
        x_copy(i).start()
    for t in range(2):
        w_copy(t).start()
    acc[...] = jnp.zeros_like(acc)
    ready[...] = jnp.zeros_like(ready)
    pool[...] = jnp.zeros_like(pool)
    lead = first_half((16, 128))
    bias = by_tower(bias_ref[0:1], bias_ref[1:2])
    own, into, _ = stitch_slabs(stitch_ref)

    def gather(row):
        line = jnp.maximum(row + 1, 0)
        for t in range(2):
            right = pltpu.roll(acc[t, 0, line], 64, 1)
            left = pltpu.roll(acc[t, 2, line], 832, 1)
            ready[t] = acc[t, 1, line] + right + left

    def finish(row):
        acts = []
        for j in range(13):
            lanes = slice(j // 2 * 128, j // 2 * 128 + 128)
            zero, one = ready[0, :, lanes], ready[1, :, lanes]
            if j % 2 == 0:
                pre_act = jnp.where(lead, zero, swap_halves(one))
            else:
                pre_act = jnp.where(lead, swap_halves(zero), one)
            act, slope = gelu_parts(pre_act + bias)
            slopes[jnp.maximum(row, 0), j] = slope.astype(BF16)
            acts.append(act)
        even = row % 2 == 0
        for q in range(6):
            total = acts[2 * q] + acts[2 * q + 1] + acts[2 * q + 2]
            pool[jnp.maximum(row + 2, 0) // 2, q] += total
            pool[jnp.maximum(row, 0) // 2, q] += jnp.where(even, total, 0.0)

    def line(i, carry):
        x_copy(i).wait()
        finish(i - 3)
        gather(i - 2)
        for t in range(2):
            weights = kernel_ref[144 * t : 144 * t + 144]
            for start in range(0, 13, 4):
                width = min(4, 13 - start)
                rows = xs[t, i, start : start + width].reshape(64 * width, 384)
                product = nt_dot(weights, rows)
                for a in range(3):
                    for b in range(3):
                        top = 16 * (3 * a + b)
                        acc[t, b, i + 2 - a, :, 64 * start : 64 * (start + width)] += product[top : top + 16]
        return carry

    def last(i, carry):
        finish(i - 3)
        gather(jnp.minimum(i - 2, 12))
        return carry

    lax.fori_loop(0, 13, line, 0)
    lax.fori_loop(13, 16, last, 0)
    for i in range(13):
        slope_copy(i).start()
    pooled = pool[1:7].reshape(36, 16, 128) * (1.0 / 9.0)
    pooled_out[...] = pooled
    pooled_copy = pltpu.make_async_copy(pooled_out, pooled_ref, out_sem.at[0])
    pooled_copy.start()
    mixed = own[None] * pooled + into[None] * swap_halves(pooled)
    flat_t = nn_dot(slab_order(0), mixed.reshape(576, 128).astype(BF16))
    flat_t_out[...] = flat_t.astype(BF16)
    flat_copy = pltpu.make_async_copy(flat_t_out, flat_t_ref, out_sem.at[1])
    flat_copy.start()
    flat = flat_t.T.astype(BF16)
    core = core_ref[0]
    copies_out = [pooled_copy, flat_copy]
    for t in range(2):
        w_copy(t).wait()
    for ref, parity in ((other_ref, 1 - core), (own_ref, core)):
        for q in range(8):
            at = pl.ds(pl.multiple_of((2 * q + parity) * 256, 256), 256)
            for t in range(2):
                ref[q, 64 * t : 64 * t + 64] = nn_dot(flat[64 * t : 64 * t + 64], ws[t, :, at]).astype(BF16)
    for i in range(13):
        slope_copy(i).wait()
    for copy in copies_out:
        copy.wait()


VMEM = pl.BlockSpec(memory_space=pltpu.VMEM)
SMEM = pl.BlockSpec(memory_space=pltpu.SMEM)
ANY = pl.BlockSpec(memory_space=pl.ANY)


def front(core, x, w, kernels, bias, stitch):
    return pl.pallas_call(
        front_kernel,
        in_specs=[SMEM, ANY, ANY, VMEM, VMEM, VMEM],
        out_specs=[ANY, ANY, ANY, VMEM, VMEM],
        out_shape=[
            jax.ShapeDtypeStruct((13, 13, 16, 128), BF16),
            jax.ShapeDtypeStruct((36, 16, 128), F32),
            jax.ShapeDtypeStruct((576, 128), BF16),
            jax.ShapeDtypeStruct((8, 128, 256), BF16),
            jax.ShapeDtypeStruct((8, 128, 256), BF16),
        ],
        scratch_shapes=[
            pltpu.VMEM((2, 13, 13, 64, 384), BF16),
            pltpu.VMEM((2, 576, 4096), BF16),
            pltpu.VMEM((2, 3, 15, 16, 896), F32),
            pltpu.VMEM((2, 16, 896), F32),
            pltpu.VMEM((8, 6, 16, 128), F32),
            pltpu.VMEM((13, 13, 16, 128), BF16),
            pltpu.VMEM((36, 16, 128), F32),
            pltpu.VMEM((576, 128), BF16),
            pltpu.SemaphoreType.DMA((13,)),
            pltpu.SemaphoreType.DMA((2,)),
            pltpu.SemaphoreType.DMA((13,)),
            pltpu.SemaphoreType.DMA((2,)),
        ],
        compiler_params=params(),
        cost_estimate=cost(10e9, 30e6),
        name="front",
    )(core, x, w, kernels, bias, stitch)


def pair_kernel(first_ref, second_ref, out_ref):
    out_ref[...] = (first_ref[...].astype(F32) + second_ref[...].astype(F32)).astype(BF16)


def pair_sum(first, second):
    return pl.pallas_call(
        pair_kernel,
        in_specs=[VMEM, VMEM],
        out_specs=VMEM,
        out_shape=jax.ShapeDtypeStruct(first.shape, BF16),
        compiler_params=params(SMALL),
        cost_estimate=cost(1e6, 2e6),
        name="pair_sum",
    )(first, second)


def hidden_kernel(counts_ref, parts_ref, bias_ref, stitch_ref, cot_ref, out_ref, grad_ref, sums_ref):
    live = counts_ref[0]
    for k in range(1, 8):
        live += counts_ref[k]
    mask = (lax.broadcasted_iota(jnp.int32, (64, 256), 0) < live).astype(F32)
    total = parts_ref[0].astype(F32)
    for k in range(1, 8):
        total += parts_ref[k].astype(F32)
    hidden, slope = [], []
    for t in range(2):
        act, der = gelu_parts(total[64 * t : 64 * t + 64] + bias_ref[t][None])
        hidden.append(act)
        slope.append(der)
    cots = [cot_ref[u].astype(F32) * mask for u in range(2)]
    stitch = [[stitch_ref[u, v][None] for v in range(2)] for u in range(2)]
    sums = []
    for u in range(2):
        out_ref[u] = (mask * (stitch[u][0] * hidden[0] + stitch[u][1] * hidden[1])).astype(BF16)
    for v in range(2):
        grad = (stitch[0][v] * cots[0] + stitch[1][v] * cots[1]) * slope[v]
        grad = grad.astype(BF16)
        for k in range(8):
            for half in range(2):
                top = 128 * half + 64 * v
                grad_ref[k, top : top + 64] = grad[:, 128 * half : 128 * half + 128]
        sums.append(jnp.sum(grad.astype(F32), axis=0, keepdims=True))
    for u in range(2):
        for v in range(2):
            sums.append(jnp.sum(cots[u] * hidden[v], axis=0, keepdims=True))
    sums_ref[...] = jnp.concatenate(sums + [jnp.zeros((2, 256), F32)], axis=0)


def hidden_layer(counts, parts, bias, stitch, cot):
    vmem = pl.BlockSpec(memory_space=pltpu.VMEM)
    return pl.pallas_call(
        hidden_kernel,
        in_specs=[pl.BlockSpec(memory_space=pltpu.SMEM), vmem, vmem, vmem, vmem],
        out_specs=[vmem, vmem, vmem],
        out_shape=[
            jax.ShapeDtypeStruct((2, 64, 256), BF16),
            jax.ShapeDtypeStruct((8, 256, 128), BF16),
            jax.ShapeDtypeStruct((8, 256), F32),
        ],
        compiler_params=params(SMALL),
        cost_estimate=cost(1e7, 3e6),
        name="hidden_layer",
    )(counts, parts, bias, stitch, cot)


def back_kernel(
    core_ref, own_ref, other_ref, w_ref, stitch_ref, pooled_ref, slope_ref,
    send_ref, pre_ref, stats_ref,
    ws, pooled, slopes, sends, w_sem, in_sem, send_sem,
):
    def w_copy(k):
        at = pl.ds(1024 * k, 1024)
        return pltpu.make_async_copy(w_ref.at[:, :, at], ws.at[:, :, at], w_sem.at[k])

    later_in = [
        pltpu.make_async_copy(pooled_ref, pooled, in_sem.at[0]),
        pltpu.make_async_copy(slope_ref, slopes, in_sem.at[1]),
    ]
    for k in range(4):
        w_copy(k).start()
    for copy in later_in:
        copy.start()
    first = core_ref[0] == 0
    perm = slab_order(1)
    own_slab, _, back_slab = stitch_slabs(stitch_ref)
    totals = [jnp.zeros((576, 128), F32)] * 2
    for k in range(4):
        w_copy(k).wait()
        blocks = []
        for q in (2 * k, 2 * k + 1):
            own, other = (jnp.concatenate([ref[q, 0:128], ref[q, 128:256]], axis=1) for ref in (own_ref, other_ref))
            blocks += [jnp.where(first, own, other), jnp.where(first, other, own)]
        rows = jnp.concatenate(blocks, axis=1)
        for t in range(2):
            totals[t] = totals[t] + nt_dot(ws[t, :, 1024 * k : 1024 * k + 1024], rows)
    flat_grad = jnp.where(first_half((576, 128)), totals[0], totals[1])
    mixed_grad = nn_dot(perm, flat_grad.astype(BF16)).reshape(36, 16, 128)
    swapped = swap_halves(mixed_grad)
    pooled_grad = own_slab[None] * mixed_grad + back_slab[None] * swapped
    pooled_grad = (pooled_grad * (1.0 / 9.0)).reshape(6, 6, 16, 128)
    for copy in later_in:
        copy.wait()
    lead = first_half((16, 128))
    bias_sum = jnp.zeros((16, 128), F32)
    zero = jnp.zeros((16, 128), F32)
    widened = []
    for p in range(6):
        line = []
        for j in range(13):
            terms = [pooled_grad[p, q] for q in range(6) if 2 * q <= j <= 2 * q + 2]
            line.append(terms[0] if len(terms) == 1 else terms[0] + terms[1])
        widened.append(line)
    copies_out = []
    for i in range(13):
        windows = [p for p in range(6) if 2 * p <= i <= 2 * p + 2]
        slabs = []
        for j in range(13):
            value = widened[windows[0]][j]
            if len(windows) == 2:
                value = value + widened[windows[1]][j]
            value = (value * slopes[i, j].astype(F32)).astype(BF16)
            pre_ref[i, j] = value
            value = value.astype(F32)
            bias_sum = bias_sum + value
            slabs.append(value)
        slabs = exchange(slabs + [zero] * 3)
        at = pl.ds(128 * i, 128)
        for m in range(16):
            block = (m % 2) * 8 + m // 2
            sends[m, :, 128 * i : 128 * i + 128] = slabs[block].astype(BF16)
        copies_out.append(pltpu.make_async_copy(sends.at[:, :, at], send_ref.at[:, :, at], send_sem.at[i]))
        copies_out[-1].start()
    pooled_in = pooled[...]
    own = jnp.sum(mixed_grad * pooled_in, axis=0)
    cross = jnp.sum(swapped * pooled_in, axis=0)
    lane = lax.broadcasted_iota(jnp.int32, (16, 128), 1)
    stats = jnp.zeros((16, 128), F32)
    for k, value in enumerate((own, cross, bias_sum)):
        for t in range(2):
            half = jnp.sum(jnp.where(lead == (t == 0), value, 0.0), axis=1, keepdims=True)
            stats = jnp.where(lane == 2 * k + t, half, stats)
    stats_ref[...] = stats
    for copy in copies_out:
        copy.wait()


def back_fc(core, own, other, w, stitch, pooled, slope):
    return pl.pallas_call(
        back_kernel,
        in_specs=[SMEM, VMEM, VMEM, ANY, VMEM, ANY, ANY],
        out_specs=[ANY, VMEM, VMEM],
        out_shape=[
            jax.ShapeDtypeStruct((16, 16, 1664), BF16),
            jax.ShapeDtypeStruct((13, 13, 16, 128), BF16),
            jax.ShapeDtypeStruct((16, 128), F32),
        ],
        scratch_shapes=[
            pltpu.VMEM((2, 576, 4096), BF16),
            pltpu.VMEM((36, 16, 128), F32),
            pltpu.VMEM((13, 13, 16, 128), BF16),
            pltpu.VMEM((16, 16, 1664), BF16),
            pltpu.SemaphoreType.DMA((4,)),
            pltpu.SemaphoreType.DMA((2,)),
            pltpu.SemaphoreType.DMA((13,)),
        ],
        compiler_params=params(),
        cost_estimate=cost(1e9, 30e6),
        name="back_fc",
    )(core, own, other, w, stitch, pooled, slope)


def weight_kernel(x_ref, pre_ref, sums_ref, stats_ref, out_ref, xs, lines, acc, x_sem):
    def x_copy(i):
        return pltpu.make_async_copy(x_ref.at[:, i], xs.at[:, i], x_sem.at[i])

    for i in range(13):
        x_copy(i).start()
    lines[...] = jnp.zeros_like(lines)
    acc[...] = jnp.zeros_like(acc)
    lead = first_half((16, 128))

    def merge(i, carry):
        zero = jnp.zeros((16, 128), F32)
        slabs = [pre_ref[i, j].astype(F32) for j in range(13)]
        turned = [swap_halves(slab) for slab in slabs]
        slabs = [zero] + slabs + [zero] * 2
        turned = [zero] + turned + [zero] * 2
        for first in range(-1, 14):
            left, right = first + 1, first + 2
            pair = (
                jnp.where(lead, slabs[left], turned[right]).astype(BF16),
                jnp.where(lead, turned[left], slabs[right]).astype(BF16),
            )
            for b in range(3):
                place = first + b - 1
                if place % 2 == 0 and 0 <= place <= 12:
                    for t in range(2):
                        lines[t, b, i + 1, :, 64 * place : 64 * place + 128] = pair[t]
        return carry

    lax.fori_loop(0, 13, merge, 0)

    def line(i, carry):
        x_copy(i).wait()
        for t in range(2):
            left = jnp.concatenate([lines[t, b, i + 2 - a] for a in range(3) for b in range(3)], axis=0)
            right = jnp.concatenate([xs[t, i].reshape(832, 384), jnp.zeros((64, 384), BF16)], axis=0)
            acc[144 * t : 144 * t + 144] += nn_dot(left, right)
        return carry

    lax.fori_loop(0, 13, line, 0)
    out_ref[0:288] = acc[...].astype(BF16)
    small = jnp.concatenate([sums_ref[...], jnp.zeros((8, 256), F32)], axis=0)
    out_ref[288:304] = jnp.concatenate([small, stats_ref[...]], axis=1).astype(BF16)


def weight_grad(x, pre, sums, stats):
    return pl.pallas_call(
        weight_kernel,
        in_specs=[ANY, VMEM, VMEM, VMEM],
        out_specs=VMEM,
        out_shape=jax.ShapeDtypeStruct((304, 384), BF16),
        scratch_shapes=[
            pltpu.VMEM((2, 13, 13, 64, 384), BF16),
            pltpu.VMEM((2, 3, 15, 16, 896), BF16),
            pltpu.VMEM((288, 384), F32),
            pltpu.SemaphoreType.DMA((13,)),
        ],
        compiler_params=params(MEDIUM),
        cost_estimate=cost(10e9, 20e6),
        name="weight_grad",
    )(x, pre, sums, stats)


def turn_kernel(place_ref, same, same_a, same_b, other, other_a, other_b, out_ref, rows):
    core, z = place_ref[0], place_ref[1]
    for parity, refs in ((core, (same, same_a, same_b)), (1 - core, (other, other_a, other_b))):
        for ref, near, first in zip(refs, (True, False, False), (0, 0, 2)):
            for k in range(ref.shape[0]):
                block = 8 * (z if near else 1 - z) + 2 * (first + k) + parity
                at = pl.ds(pl.multiple_of(16 * block, 16), 16)
                for tap in range(9):
                    rows[tap, at] = ref[k, core, 16 * tap : 16 * tap + 16]
    for tap in range(9):
        out_ref[:, 256 * tap : 256 * tap + 256] = rows[tap].T


def turned(place, parts):
    return pl.pallas_call(
        turn_kernel,
        in_specs=[SMEM] + [VMEM] * 6,
        out_specs=VMEM,
        out_shape=jax.ShapeDtypeStruct((384, 2304), BF16),
        scratch_shapes=[pltpu.VMEM((9, 256, 384), BF16)],
        compiler_params=params(SMALL),
        cost_estimate=cost(1e9, 4e6),
        name="turned_kernels",
    )(place, *parts)


def input_kernel(g_ref, w_ref, out_ref, taps):
    zero = jnp.zeros((256, 128), BF16)
    for b in range(3):
        taps[b, :, 0:128] = zero
        taps[b, :, 1792:1920] = zero

    def widen(i):
        row = g_ref[:, :, 128 * i : 128 * i + 128].reshape(256, 128)
        at = slice(128 * i + 128, 128 * i + 256)
        taps[1, :, at] = row
        row = row.astype(F32)
        taps[0, :, at] = pltpu.roll(row, 120, 1).astype(BF16)
        taps[2, :, at] = pltpu.roll(row, 8, 1).astype(BF16)

    for i in range(3):
        widen(i)
    weights = w_ref[...]
    for start in range(0, 13, 2):
        width = 128 * min(2, 13 - start)
        right = jnp.concatenate(
            [
                taps[b, :, 128 * (start + 2 - a) : 128 * (start + 2 - a) + width]
                for a in range(3)
                for b in range(3)
            ],
            axis=0,
        )
        for i in range(start + 3, min(start + 5, 13)):
            widen(i)
        product = nn_dot(weights, right)
        for m in range(16):
            out_ref[m, :, 128 * start : 128 * start + width] = product[24 * m : 24 * m + 24].astype(BF16)


def input_grad_part(g, w):
    return pl.pallas_call(
        input_kernel,
        in_specs=[VMEM, VMEM],
        out_specs=VMEM,
        out_shape=jax.ShapeDtypeStruct((16, 24, 1664), BF16),
        scratch_shapes=[pltpu.VMEM((3, 256, 1920), BF16)],
        compiler_params=params(SMALL),
        cost_estimate=cost(4e9, 4e6),
        name="input_grad",
    )(g, w)


def place_kernel(part_ref, out_ref, rows, sem):
    copies = [pltpu.make_async_copy(rows.at[:, i], out_ref.at[:, i], sem.at[i]) for i in range(13)]
    for i in range(13):
        lanes = slice(128 * i, 128 * i + 128)
        slabs = [part_ref[2 * (block % 8) + block // 8, :, lanes].astype(F32) for block in range(16)]
        slabs = exchange(slabs)
        for j in range(13):
            rows[0, i, j] = slabs[j][:, 0:64].astype(BF16)
            rows[1, i, j] = swap_halves(slabs[j])[:, 0:64].astype(BF16)
        copies[i].start()
    for copy in copies:
        copy.wait()


def placed_back(parts):
    return pl.pallas_call(
        place_kernel,
        in_specs=[VMEM],
        out_specs=ANY,
        out_shape=jax.ShapeDtypeStruct((2, 13, 13, 24, 64), BF16),
        scratch_shapes=[pltpu.VMEM((2, 13, 13, 24, 64), BF16), pltpu.SemaphoreType.DMA((13,))],
        compiler_params=params(SMALL),
        cost_estimate=cost(1e8, 3e6),
        name="placed_back",
    )(parts)


def fc_weight_kernel(place_ref, flat_0, flat_1, flat_3, flat_2, own_ref, other_ref, out_ref):
    core = place_ref[0]
    lead = first_half((576, 128))
    zero = jnp.zeros((576, 128), BF16)
    flats = [ref[h] for ref in (flat_0, flat_1, flat_3, flat_2) for h in range(2)]
    lefts = [
        jnp.concatenate([jnp.where(lead, flat, zero) for flat in flats], axis=1),
        jnp.concatenate([jnp.where(lead, zero, flat) for flat in flats], axis=1),
    ]
    for ref, parity in ((own_ref, core), (other_ref, 1 - core)):
        for half in range(2):
            right = jnp.concatenate(
                [ref[place_ref[1 + k], 128 * half : 128 * half + 128] for k in range(8)], axis=0
            )
            at = pl.ds(pl.multiple_of(parity * 256 + 128 * half, 128), 128)
            for t in range(2):
                out_ref[t, :, at] = nn_dot(lefts[t], right)


def fc_weight_grad_of(place, flats, own, other):
    return pl.pallas_call(
        fc_weight_kernel,
        in_specs=[SMEM] + [VMEM] * 6,
        out_specs=VMEM,
        out_shape=jax.ShapeDtypeStruct((2, 576, 512), F32),
        compiler_params=params(SMALL),
        cost_estimate=cost(3e9, 5e6),
        name="fc_weight_grad",
    )(place, *flats, own, other)


def row_of(column):
    size = column.shape[0]
    eye = lax.broadcasted_iota(jnp.int32, (size, size), 0) == lax.broadcasted_iota(jnp.int32, (size, size), 1)
    return jnp.sum(jnp.where(eye, column, 0.0), axis=0, keepdims=True)


def total_kernel(part_0, part_1, part_2, part_3, conv_ref, bias_ref, first_ref, fc_bias_ref, second_ref):
    total = (part_0[...].astype(F32) + part_1[...].astype(F32)) + (part_2[...].astype(F32) + part_3[...].astype(F32))
    conv_ref[...] = total[0:288]
    for t in range(2):
        fc_bias_ref[t : t + 1] = total[288 + t : 289 + t, 0:256]
        bias_ref[t : t + 1] = row_of(total[288:304, 260 + t : 261 + t])
    for u in range(2):
        for v in range(2):
            line = 290 + 2 * u + v
            second_ref[u, v : v + 1] = total[line : line + 1, 0:256]
            place = 256 + u if u == v else 258 + v
            first_ref[u, v : v + 1] = row_of(total[288:304, place : place + 1])


def summed(parts):
    return pl.pallas_call(
        total_kernel,
        in_specs=[VMEM] * 4,
        out_specs=[VMEM] * 5,
        out_shape=[
            jax.ShapeDtypeStruct((288, 384), F32),
            jax.ShapeDtypeStruct((2, 16), F32),
            jax.ShapeDtypeStruct((2, 2, 16), F32),
            jax.ShapeDtypeStruct((2, 256), F32),
            jax.ShapeDtypeStruct((2, 2, 256), F32),
        ],
        compiler_params=params(SMALL),
        cost_estimate=cost(1e7, 3e6),
        name="summed",
    )(*parts)


def mp_moves(z_step, y_step, core_step):
    return [
        ((z * 4 + y) * 2 + c, (((z + z_step) % 2) * 4 + (y + y_step) % 4) * 2 + (c + core_step) % 2)
        for z in range(2)
        for y in range(4)
        for c in range(2)
    ]


def dp_moves(x_step, z_step):
    return [(x * 2 + h, ((x + x_step) % 4) * 2 + (h + z_step) % 2) for x in range(4) for h in range(2)]


SAME_CORE = [[2 * k + c for k in range(8)] for c in range(2)]
SAME_Z_CORE = [[8 * z + 2 * y + c for y in range(4)] for z in range(2) for c in range(2)]


def over_mp(array, z_step=0, y_step=0, core_step=0):
    return lax.ppermute(array, "mp", mp_moves(z_step, y_step, core_step))


def over_dp(array, x_step=0, z_step=0):
    return lax.ppermute(array, "dp", dp_moves(x_step, z_step))


def over_far_z(array):
    moves = [
        (((z * 4 + y) * 2 + c) * 8 + x * 2 + h, (((1 - z) * 4 + y) * 2 + c) * 8 + x * 2 + 1 - h)
        for z in range(2)
        for y in range(4)
        for c in range(2)
        for x in range(4)
        for h in range(2)
    ]
    return lax.ppermute(array, ("mp", "dp"), moves)


def dealt(array, groups=None, axis="mp"):
    return lax.all_to_all(array, axis, 0, 0, tiled=True, axis_index_groups=groups)


def pick(array, index, axis):
    return lax.dynamic_index_in_dim(array, index, axis, keepdims=False)


def local(
    inputs,
    conv_weight,
    conv_bias,
    first_stitch,
    fc_weight,
    fc_bias,
    second_stitch,
    crop_counts,
    out_grad,
):
    x = jnp.transpose(inputs, (0, 2, 3, 1, 4))
    kernels = jnp.transpose(conv_weight, (0, 1, 2, 4, 3)).reshape(2, 144, 384)
    stitch_one = jnp.transpose(first_stitch, (1, 2, 0))
    mp_at, dp_at = lax.axis_index("mp"), lax.axis_index("dp")
    z_at, y_at, core = mp_at // 8, (mp_at // 2) % 4, mp_at % 2
    x_at, h_at = dp_at // 2, dp_at % 2
    core_arg = core.astype(jnp.int32).reshape(1)

    blocks = dealt(jnp.broadcast_to(kernels[None], (4, 2, 144, 384)), SAME_Z_CORE)
    slope, pooled, flat_t, own, other = front(
        core_arg, x, fc_weight, kernels.reshape(288, 384), conv_bias, stitch_one
    )
    own, blocks = lax.optimization_barrier((own, blocks))
    own = pair_sum(own, over_mp(other, core_step=1))
    parts = dealt(own, SAME_CORE)

    flat_z = over_dp(flat_t, z_step=1)
    blocks_a, blocks_b = over_mp(blocks[0:2], z_step=1), over_far_z(blocks[2:4])
    output, grad_copies, sums = hidden_layer(
        crop_counts,
        parts,
        fc_bias.T,
        jnp.transpose(second_stitch, (1, 2, 0)),
        jnp.transpose(out_grad, (1, 2, 0)),
    )
    grads_own = dealt(grad_copies, SAME_CORE)
    same = [blocks, blocks_a, blocks_b]
    kernels_all = turned(
        jnp.stack([core, z_at]).astype(jnp.int32), same + [over_mp(part, core_step=1) for part in same]
    )
    flat_pair = jnp.stack([flat_t, flat_z])
    flat_1, flat_3 = over_dp(flat_pair, x_step=1), over_dp(flat_pair, x_step=3)
    grads_own, flat_1, flat_3, kernels_all = lax.optimization_barrier((grads_own, flat_1, flat_3, kernels_all))
    grads_other = over_mp(grads_own, core_step=1)
    flats = [flat_pair, flat_1, flat_3, over_dp(flat_pair, x_step=2)]
    slice_own = dealt(grads_own, axis="dp")
    send, pre, stats = back_fc(core_arg, grads_own, grads_other, fc_weight, stitch_one, pooled, slope)
    send, slice_own = lax.optimization_barrier((send, slice_own))
    slice_other = over_mp(slice_own, core_step=1)
    pre_all = dealt(send)

    weight_part = weight_grad(x, pre, sums, stats)
    weight_z = over_dp(weight_part, z_step=1)
    pre_all, weight_part = lax.optimization_barrier((pre_all, weight_part))
    input_part = input_grad_part(pre_all, kernels_all)
    input_part, weight_z = lax.optimization_barrier((input_part, weight_z))
    part = dealt(input_part)

    weight_pair = pair_sum(weight_part, weight_z)
    conv_sum, conv_bias_grad, first_sum, fc_bias_sum, second_sum = summed(
        [weight_pair] + [over_dp(weight_pair, x_step=k) for k in range(1, 4)]
    )
    crops_place = jnp.stack(
        [core] + [(x_at + 4 - k) % 4 * 2 + (h_at + dh) % 2 for k in (0, 1, 3, 2) for dh in range(2)]
    ).astype(jnp.int32)
    fc_weight_grad = fc_weight_grad_of(crops_place, flats, slice_own, slice_other)
    input_grad = jnp.transpose(placed_back(part), (0, 4, 1, 2, 3))

    conv_weight_grad = jnp.transpose(conv_sum.reshape(2, 3, 3, 16, 384), (0, 1, 2, 4, 3))
    first_stitch_grad = jnp.transpose(first_sum, (2, 0, 1))
    fc_bias_grad = fc_bias_sum.T
    second_stitch_grad = jnp.transpose(second_sum, (2, 0, 1))
    return (
        jnp.transpose(output, (2, 0, 1)),
        input_grad,
        conv_weight_grad,
        conv_bias_grad,
        first_stitch_grad,
        fc_weight_grad,
        fc_bias_grad,
        second_stitch_grad,
    )


def solution(mesh):
    placed = (
        P(None, "dp", None, None, None),
        P(None, None, None, None, "mp"),
        P(None, "mp"),
        P("mp", None, None),
        P(None, "mp", None),
        P("mp", None),
        P("mp", None, None),
        P("dp"),
        P("mp", None, "dp"),
    )
    return jax.shard_map(
        local,
        mesh=mesh,
        in_specs=placed,
        out_specs=(
            P("mp", None, "dp"),
            P(None, "dp", None, None, "mp"),
            P(None, None, None, None, "mp"),
            P(None, "mp"),
            P("mp", None, None),
            P(None, "mp", "dp"),
            P("mp", None),
            P("mp", None, None),
        ),
        check_vma=False,
    )
```

```python
import jax
import jax.numpy as jnp
from jax import lax
from jax.experimental import pallas as pl
from jax.experimental.pallas import tpu as pltpu
from jax.sharding import PartitionSpec as P

F32 = jnp.float32
BF16 = jnp.bfloat16
LARGE, MEDIUM, SMALL = 56, 50, 16


def params(mib=LARGE):
    return pltpu.CompilerParams(vmem_limit_bytes=mib * 1024 * 1024)


def cost(flops, read):
    return pl.CostEstimate(flops=int(flops), bytes_accessed=int(read), transcendentals=0)


def nt_dot(left, right):
    return lax.dot_general(left, right, (((1,), (1,)), ((), ())), preferred_element_type=F32)


def nn_dot(left, right):
    return lax.dot_general(left, right, (((1,), (0,)), ((), ())), preferred_element_type=F32)


def first_half(shape):
    return lax.broadcasted_iota(jnp.int32, shape, len(shape) - 1) < 64


def swap_halves(value):
    return pltpu.roll(value, 64, value.ndim - 1)


def gelu_parts(x):
    root, cubic = 0.7978845608028654, 0.044715
    square = x * x
    tanh = jnp.tanh(root * x * (1.0 + cubic * square))
    half = 0.5 + 0.5 * tanh
    slope = half + 0.5 * x * (1.0 - tanh * tanh) * (root * (1.0 + 3.0 * cubic * square))
    return x * half, slope


def spread(slabs):
    lane = lax.broadcasted_iota(jnp.int32, slabs[0].shape, 1)
    for bit in range(4):
        odd = (lane & (8 << bit)) != 0
        slabs = [jnp.where(odd, slabs[(k + (1 << bit)) % 16], slabs[k]) for k in range(16)]
    return slabs


def exchange(slabs):
    slabs = spread(slabs)
    slabs = [slabs[0]] + [pltpu.roll(slabs[k], 8 * k, 1) for k in range(1, 16)]
    slabs = spread(slabs)
    return [slabs[-k % 16] for k in range(16)]


def column(row):
    size = row.shape[1]
    eye = lax.broadcasted_iota(jnp.int32, (size, size), 0) == lax.broadcasted_iota(jnp.int32, (size, size), 1)
    return jnp.sum(jnp.where(eye, row, 0.0), axis=1, keepdims=True)


def by_tower(first, second):
    lead = first_half((16, 128))
    return jnp.where(lead, column(first), column(second))


def stitch_slabs(stitch_ref):
    part = [[stitch_ref[u, v : v + 1] for v in range(2)] for u in range(2)]
    own = by_tower(part[0][0], part[1][1])
    into = by_tower(part[0][1], part[1][0])
    back = by_tower(part[1][0], part[0][1])
    return own, into, back


def slab_order(fc_axis):
    fc_row = lax.broadcasted_iota(jnp.int32, (576, 576), fc_axis)
    slab_row = lax.broadcasted_iota(jnp.int32, (576, 576), 1 - fc_axis)
    return (fc_row == 36 * (slab_row & 15) + (slab_row >> 4)).astype(F32).astype(BF16)


def front_kernel(
    core_ref, x_ref, w_ref, kernel_ref, bias_ref, stitch_ref,
    slope_ref, pooled_ref, flat_t_ref, own_ref, other_ref,
    xs, ws, acc, ready, pool, slopes, pooled_out, flat_t_out, x_sem, w_sem, slope_sem, out_sem,
):
    def x_copy(i):
        return pltpu.make_async_copy(x_ref.at[:, i], xs.at[:, i], x_sem.at[i])

    def w_copy(t):
        return pltpu.make_async_copy(w_ref.at[t], ws.at[t], w_sem.at[t])

    def slope_copy(i):
        return pltpu.make_async_copy(slopes.at[i], slope_ref.at[i], slope_sem.at[i])

    for i in range(13):
        x_copy(i).start()
    for t in range(2):
        w_copy(t).start()
    acc[...] = jnp.zeros_like(acc)
    ready[...] = jnp.zeros_like(ready)
    pool[...] = jnp.zeros_like(pool)
    lead = first_half((16, 128))
    bias = by_tower(bias_ref[0:1], bias_ref[1:2])
    own, into, _ = stitch_slabs(stitch_ref)

    def gather(row):
        line = jnp.maximum(row + 1, 0)
        for t in range(2):
            right = pltpu.roll(acc[t, 0, line], 64, 1)
            left = pltpu.roll(acc[t, 2, line], 832, 1)
            ready[t] = acc[t, 1, line] + right + left

    def finish(row):
        acts = []
        for j in range(13):
            lanes = slice(j // 2 * 128, j // 2 * 128 + 128)
            zero, one = ready[0, :, lanes], ready[1, :, lanes]
            if j % 2 == 0:
                pre_act = jnp.where(lead, zero, swap_halves(one))
            else:
                pre_act = jnp.where(lead, swap_halves(zero), one)
            act, slope = gelu_parts(pre_act + bias)
            slopes[jnp.maximum(row, 0), j] = slope.astype(BF16)
            acts.append(act)
        even = row % 2 == 0
        for q in range(6):
            total = acts[2 * q] + acts[2 * q + 1] + acts[2 * q + 2]
            pool[jnp.maximum(row + 2, 0) // 2, q] += total
            pool[jnp.maximum(row, 0) // 2, q] += jnp.where(even, total, 0.0)

    def line(i, carry):
        x_copy(i).wait()
        finish(i - 3)
        gather(i - 2)
        for t in range(2):
            weights = kernel_ref[144 * t : 144 * t + 144]
            for start in range(0, 13, 4):
                width = min(4, 13 - start)
                rows = xs[t, i, start : start + width].reshape(64 * width, 384)
                product = nt_dot(weights, rows)
                for a in range(3):
                    for b in range(3):
                        top = 16 * (3 * a + b)
                        acc[t, b, i + 2 - a, :, 64 * start : 64 * (start + width)] += product[top : top + 16]
        return carry

    def last(i, carry):
        finish(i - 3)
        gather(jnp.minimum(i - 2, 12))
        return carry

    lax.fori_loop(0, 13, line, 0)
    lax.fori_loop(13, 16, last, 0)
    for i in range(13):
        slope_copy(i).start()
    pooled = pool[1:7].reshape(36, 16, 128) * (1.0 / 9.0)
    pooled_out[...] = pooled
    pooled_copy = pltpu.make_async_copy(pooled_out, pooled_ref, out_sem.at[0])
    pooled_copy.start()
    mixed = own[None] * pooled + into[None] * swap_halves(pooled)
    flat_t = nn_dot(slab_order(0), mixed.reshape(576, 128).astype(BF16))
    flat_t_out[...] = flat_t.astype(BF16)
    flat_copy = pltpu.make_async_copy(flat_t_out, flat_t_ref, out_sem.at[1])
    flat_copy.start()
    flat = flat_t.T.astype(BF16)
    core = core_ref[0]
    copies_out = [pooled_copy, flat_copy]
    for t in range(2):
        w_copy(t).wait()
    for ref, parity in ((other_ref, 1 - core), (own_ref, core)):
        for q in range(8):
            at = pl.ds(pl.multiple_of((2 * q + parity) * 256, 256), 256)
            for t in range(2):
                ref[q, 64 * t : 64 * t + 64] = nn_dot(flat[64 * t : 64 * t + 64], ws[t, :, at]).astype(BF16)
    for i in range(13):
        slope_copy(i).wait()
    for copy in copies_out:
        copy.wait()


VMEM = pl.BlockSpec(memory_space=pltpu.VMEM)
SMEM = pl.BlockSpec(memory_space=pltpu.SMEM)
ANY = pl.BlockSpec(memory_space=pl.ANY)


def front(core, x, w, kernels, bias, stitch):
    return pl.pallas_call(
        front_kernel,
        in_specs=[SMEM, ANY, ANY, VMEM, VMEM, VMEM],
        out_specs=[ANY, ANY, ANY, VMEM, VMEM],
        out_shape=[
            jax.ShapeDtypeStruct((13, 13, 16, 128), BF16),
            jax.ShapeDtypeStruct((36, 16, 128), F32),
            jax.ShapeDtypeStruct((576, 128), BF16),
            jax.ShapeDtypeStruct((8, 128, 256), BF16),
            jax.ShapeDtypeStruct((8, 128, 256), BF16),
        ],
        scratch_shapes=[
            pltpu.VMEM((2, 13, 13, 64, 384), BF16),
            pltpu.VMEM((2, 576, 4096), BF16),
            pltpu.VMEM((2, 3, 15, 16, 896), F32),
            pltpu.VMEM((2, 16, 896), F32),
            pltpu.VMEM((8, 6, 16, 128), F32),
            pltpu.VMEM((13, 13, 16, 128), BF16),
            pltpu.VMEM((36, 16, 128), F32),
            pltpu.VMEM((576, 128), BF16),
            pltpu.SemaphoreType.DMA((13,)),
            pltpu.SemaphoreType.DMA((2,)),
            pltpu.SemaphoreType.DMA((13,)),
            pltpu.SemaphoreType.DMA((2,)),
        ],
        compiler_params=params(),
        cost_estimate=cost(10e9, 30e6),
        name="front",
    )(core, x, w, kernels, bias, stitch)


def pair_kernel(first_ref, second_ref, out_ref):
    out_ref[...] = (first_ref[...].astype(F32) + second_ref[...].astype(F32)).astype(BF16)


def pair_sum(first, second):
    return pl.pallas_call(
        pair_kernel,
        in_specs=[VMEM, VMEM],
        out_specs=VMEM,
        out_shape=jax.ShapeDtypeStruct(first.shape, BF16),
        compiler_params=params(SMALL),
        cost_estimate=cost(1e6, 2e6),
        name="pair_sum",
    )(first, second)


def hidden_kernel(counts_ref, parts_ref, bias_ref, stitch_ref, cot_ref, out_ref, grad_ref, sums_ref):
    live = counts_ref[0]
    for k in range(1, 8):
        live += counts_ref[k]
    mask = (lax.broadcasted_iota(jnp.int32, (64, 256), 0) < live).astype(F32)
    total = parts_ref[0].astype(F32)
    for k in range(1, 8):
        total += parts_ref[k].astype(F32)
    hidden, slope = [], []
    for t in range(2):
        act, der = gelu_parts(total[64 * t : 64 * t + 64] + bias_ref[t][None])
        hidden.append(act)
        slope.append(der)
    cots = [cot_ref[u].astype(F32) * mask for u in range(2)]
    stitch = [[stitch_ref[u, v][None] for v in range(2)] for u in range(2)]
    sums = []
    for u in range(2):
        out_ref[u] = (mask * (stitch[u][0] * hidden[0] + stitch[u][1] * hidden[1])).astype(BF16)
    for v in range(2):
        grad = (stitch[0][v] * cots[0] + stitch[1][v] * cots[1]) * slope[v]
        grad = grad.astype(BF16)
        for k in range(8):
            for half in range(2):
                top = 128 * half + 64 * v
                grad_ref[k, top : top + 64] = grad[:, 128 * half : 128 * half + 128]
        sums.append(jnp.sum(grad.astype(F32), axis=0, keepdims=True))
    for u in range(2):
        for v in range(2):
            sums.append(jnp.sum(cots[u] * hidden[v], axis=0, keepdims=True))
    sums_ref[...] = jnp.concatenate(sums + [jnp.zeros((2, 256), F32)], axis=0)


def hidden_layer(counts, parts, bias, stitch, cot):
    vmem = pl.BlockSpec(memory_space=pltpu.VMEM)
    return pl.pallas_call(
        hidden_kernel,
        in_specs=[pl.BlockSpec(memory_space=pltpu.SMEM), vmem, vmem, vmem, vmem],
        out_specs=[vmem, vmem, vmem],
        out_shape=[
            jax.ShapeDtypeStruct((2, 64, 256), BF16),
            jax.ShapeDtypeStruct((8, 256, 128), BF16),
            jax.ShapeDtypeStruct((8, 256), F32),
        ],
        compiler_params=params(SMALL),
        cost_estimate=cost(1e7, 3e6),
        name="hidden_layer",
    )(counts, parts, bias, stitch, cot)


def back_kernel(
    core_ref, own_ref, other_ref, w_ref, stitch_ref, pooled_ref, slope_ref,
    send_ref, pre_ref, stats_ref,
    ws, pooled, slopes, sends, w_sem, in_sem, send_sem,
):
    def w_copy(k):
        at = pl.ds(1024 * k, 1024)
        return pltpu.make_async_copy(w_ref.at[:, :, at], ws.at[:, :, at], w_sem.at[k])

    later_in = [
        pltpu.make_async_copy(pooled_ref, pooled, in_sem.at[0]),
        pltpu.make_async_copy(slope_ref, slopes, in_sem.at[1]),
    ]
    for k in range(4):
        w_copy(k).start()
    for copy in later_in:
        copy.start()
    first = core_ref[0] == 0
    perm = slab_order(1)
    own_slab, _, back_slab = stitch_slabs(stitch_ref)
    totals = [jnp.zeros((576, 128), F32)] * 2
    for k in range(4):
        w_copy(k).wait()
        blocks = []
        for q in (2 * k, 2 * k + 1):
            own, other = (jnp.concatenate([ref[q, 0:128], ref[q, 128:256]], axis=1) for ref in (own_ref, other_ref))
            blocks += [jnp.where(first, own, other), jnp.where(first, other, own)]
        rows = jnp.concatenate(blocks, axis=1)
        for t in range(2):
            totals[t] = totals[t] + nt_dot(ws[t, :, 1024 * k : 1024 * k + 1024], rows)
    flat_grad = jnp.where(first_half((576, 128)), totals[0], totals[1])
    mixed_grad = nn_dot(perm, flat_grad.astype(BF16)).reshape(36, 16, 128)
    swapped = swap_halves(mixed_grad)
    pooled_grad = own_slab[None] * mixed_grad + back_slab[None] * swapped
    pooled_grad = (pooled_grad * (1.0 / 9.0)).reshape(6, 6, 16, 128)
    for copy in later_in:
        copy.wait()
    lead = first_half((16, 128))
    bias_sum = jnp.zeros((16, 128), F32)
    zero = jnp.zeros((16, 128), F32)
    widened = []
    for p in range(6):
        line = []
        for j in range(13):
            terms = [pooled_grad[p, q] for q in range(6) if 2 * q <= j <= 2 * q + 2]
            line.append(terms[0] if len(terms) == 1 else terms[0] + terms[1])
        widened.append(line)
    copies_out = []
    for i in range(13):
        windows = [p for p in range(6) if 2 * p <= i <= 2 * p + 2]
        slabs = []
        for j in range(13):
            value = widened[windows[0]][j]
            if len(windows) == 2:
                value = value + widened[windows[1]][j]
            value = (value * slopes[i, j].astype(F32)).astype(BF16)
            pre_ref[i, j] = value
            value = value.astype(F32)
            bias_sum = bias_sum + value
            slabs.append(value)
        slabs = exchange(slabs + [zero] * 3)
        at = pl.ds(128 * i, 128)
        for m in range(16):
            block = (m % 2) * 8 + m // 2
            sends[m, :, 128 * i : 128 * i + 128] = slabs[block].astype(BF16)
        copies_out.append(pltpu.make_async_copy(sends.at[:, :, at], send_ref.at[:, :, at], send_sem.at[i]))
        copies_out[-1].start()
    pooled_in = pooled[...]
    own = jnp.sum(mixed_grad * pooled_in, axis=0)
    cross = jnp.sum(swapped * pooled_in, axis=0)
    lane = lax.broadcasted_iota(jnp.int32, (16, 128), 1)
    stats = jnp.zeros((16, 128), F32)
    for k, value in enumerate((own, cross, bias_sum)):
        for t in range(2):
            half = jnp.sum(jnp.where(lead == (t == 0), value, 0.0), axis=1, keepdims=True)
            stats = jnp.where(lane == 2 * k + t, half, stats)
    stats_ref[...] = stats
    for copy in copies_out:
        copy.wait()


def back_fc(core, own, other, w, stitch, pooled, slope):
    return pl.pallas_call(
        back_kernel,
        in_specs=[SMEM, VMEM, VMEM, ANY, VMEM, ANY, ANY],
        out_specs=[ANY, VMEM, VMEM],
        out_shape=[
            jax.ShapeDtypeStruct((16, 16, 1664), BF16),
            jax.ShapeDtypeStruct((13, 13, 16, 128), BF16),
            jax.ShapeDtypeStruct((16, 128), F32),
        ],
        scratch_shapes=[
            pltpu.VMEM((2, 576, 4096), BF16),
            pltpu.VMEM((36, 16, 128), F32),
            pltpu.VMEM((13, 13, 16, 128), BF16),
            pltpu.VMEM((16, 16, 1664), BF16),
            pltpu.SemaphoreType.DMA((4,)),
            pltpu.SemaphoreType.DMA((2,)),
            pltpu.SemaphoreType.DMA((13,)),
        ],
        compiler_params=params(),
        cost_estimate=cost(1e9, 30e6),
        name="back_fc",
    )(core, own, other, w, stitch, pooled, slope)


def weight_kernel(x_ref, pre_ref, sums_ref, stats_ref, out_ref, xs, lines, acc, x_sem):
    def x_copy(i):
        return pltpu.make_async_copy(x_ref.at[:, i], xs.at[:, i], x_sem.at[i])

    for i in range(13):
        x_copy(i).start()
    lines[...] = jnp.zeros_like(lines)
    acc[...] = jnp.zeros_like(acc)
    lead = first_half((16, 128))

    def merge(i, carry):
        zero = jnp.zeros((16, 128), F32)
        slabs = [pre_ref[i, j].astype(F32) for j in range(13)]
        turned = [swap_halves(slab) for slab in slabs]
        slabs = [zero] + slabs + [zero] * 2
        turned = [zero] + turned + [zero] * 2
        for first in range(-1, 14):
            left, right = first + 1, first + 2
            pair = (
                jnp.where(lead, slabs[left], turned[right]).astype(BF16),
                jnp.where(lead, turned[left], slabs[right]).astype(BF16),
            )
            for b in range(3):
                place = first + b - 1
                if place % 2 == 0 and 0 <= place <= 12:
                    for t in range(2):
                        lines[t, b, i + 1, :, 64 * place : 64 * place + 128] = pair[t]
        return carry

    lax.fori_loop(0, 13, merge, 0)

    def line(i, carry):
        x_copy(i).wait()
        for t in range(2):
            left = jnp.concatenate([lines[t, b, i + 2 - a] for a in range(3) for b in range(3)], axis=0)
            right = jnp.concatenate([xs[t, i].reshape(832, 384), jnp.zeros((64, 384), BF16)], axis=0)
            acc[144 * t : 144 * t + 144] += nn_dot(left, right)
        return carry

    lax.fori_loop(0, 13, line, 0)
    out_ref[0:288] = acc[...].astype(BF16)
    small = jnp.concatenate([sums_ref[...], jnp.zeros((8, 256), F32)], axis=0)
    out_ref[288:304] = jnp.concatenate([small, stats_ref[...]], axis=1).astype(BF16)


def weight_grad(x, pre, sums, stats):
    return pl.pallas_call(
        weight_kernel,
        in_specs=[ANY, VMEM, VMEM, VMEM],
        out_specs=VMEM,
        out_shape=jax.ShapeDtypeStruct((304, 384), BF16),
        scratch_shapes=[
            pltpu.VMEM((2, 13, 13, 64, 384), BF16),
            pltpu.VMEM((2, 3, 15, 16, 896), BF16),
            pltpu.VMEM((288, 384), F32),
            pltpu.SemaphoreType.DMA((13,)),
        ],
        compiler_params=params(MEDIUM),
        cost_estimate=cost(10e9, 20e6),
        name="weight_grad",
    )(x, pre, sums, stats)


def turn_kernel(place_ref, *refs):
    out_ref, rows = refs[8:]
    core, z, y = place_ref[0], place_ref[1], place_ref[2]
    for parity, group in ((core, refs[0:4]), (1 - core, refs[4:8])):
        for part, ref in enumerate(group):
            for k in range(2):
                from_y = lax.rem(y + 4 - (2 * (part % 2) + k), 4)
                block = 8 * (z if part < 2 else 1 - z) + 2 * from_y + parity
                at = pl.ds(pl.multiple_of(16 * block, 16), 16)
                for tap in range(9):
                    rows[tap, at] = ref[k, core, 16 * tap : 16 * tap + 16]
    for tap in range(9):
        out_ref[:, 256 * tap : 256 * tap + 256] = rows[tap].T


def turned(place, parts):
    return pl.pallas_call(
        turn_kernel,
        in_specs=[SMEM] + [VMEM] * 8,
        out_specs=VMEM,
        out_shape=jax.ShapeDtypeStruct((384, 2304), BF16),
        scratch_shapes=[pltpu.VMEM((9, 256, 384), BF16)],
        compiler_params=params(63),
        cost_estimate=cost(1e9, 4e6),
        name="turned_kernels",
    )(place, *parts)


def input_kernel(g_ref, w_ref, out_ref, taps):
    zero = jnp.zeros((256, 128), BF16)
    for b in range(3):
        taps[b, :, 0:128] = zero
        taps[b, :, 1792:1920] = zero

    def widen(i):
        row = g_ref[:, :, 128 * i : 128 * i + 128].reshape(256, 128)
        at = slice(128 * i + 128, 128 * i + 256)
        taps[1, :, at] = row
        row = row.astype(F32)
        taps[0, :, at] = pltpu.roll(row, 120, 1).astype(BF16)
        taps[2, :, at] = pltpu.roll(row, 8, 1).astype(BF16)

    for i in range(3):
        widen(i)
    weights = w_ref[...]
    for start in range(0, 13, 2):
        width = 128 * min(2, 13 - start)
        right = jnp.concatenate(
            [
                taps[b, :, 128 * (start + 2 - a) : 128 * (start + 2 - a) + width]
                for a in range(3)
                for b in range(3)
            ],
            axis=0,
        )
        for i in range(start + 3, min(start + 5, 13)):
            widen(i)
        product = nn_dot(weights, right)
        for m in range(16):
            out_ref[m, :, 128 * start : 128 * start + width] = product[24 * m : 24 * m + 24].astype(BF16)


def input_grad_part(g, w):
    return pl.pallas_call(
        input_kernel,
        in_specs=[VMEM, VMEM],
        out_specs=VMEM,
        out_shape=jax.ShapeDtypeStruct((16, 24, 1664), BF16),
        scratch_shapes=[pltpu.VMEM((3, 256, 1920), BF16)],
        compiler_params=params(SMALL),
        cost_estimate=cost(4e9, 4e6),
        name="input_grad",
    )(g, w)


def place_kernel(part_ref, out_ref, rows, sem):
    copies = [pltpu.make_async_copy(rows.at[:, i], out_ref.at[:, i], sem.at[i]) for i in range(13)]
    for i in range(13):
        lanes = slice(128 * i, 128 * i + 128)
        slabs = [part_ref[2 * (block % 8) + block // 8, :, lanes].astype(F32) for block in range(16)]
        slabs = exchange(slabs)
        for j in range(13):
            rows[0, i, j] = slabs[j][:, 0:64].astype(BF16)
            rows[1, i, j] = swap_halves(slabs[j])[:, 0:64].astype(BF16)
        copies[i].start()
    for copy in copies:
        copy.wait()


def placed_back(parts):
    return pl.pallas_call(
        place_kernel,
        in_specs=[VMEM],
        out_specs=ANY,
        out_shape=jax.ShapeDtypeStruct((2, 13, 13, 24, 64), BF16),
        scratch_shapes=[pltpu.VMEM((2, 13, 13, 24, 64), BF16), pltpu.SemaphoreType.DMA((13,))],
        compiler_params=params(SMALL),
        cost_estimate=cost(1e8, 3e6),
        name="placed_back",
    )(parts)


def fc_weight_kernel(place_ref, flat_0, flat_1, flat_3, flat_2, own_ref, other_ref, out_ref):
    core = place_ref[0]
    lead = first_half((576, 128))
    zero = jnp.zeros((576, 128), BF16)
    flats = [ref[h] for ref in (flat_0, flat_1, flat_3, flat_2) for h in range(2)]
    lefts = [
        jnp.concatenate([jnp.where(lead, flat, zero) for flat in flats], axis=1),
        jnp.concatenate([jnp.where(lead, zero, flat) for flat in flats], axis=1),
    ]
    for ref, parity in ((own_ref, core), (other_ref, 1 - core)):
        for half in range(2):
            right = jnp.concatenate(
                [ref[place_ref[1 + k], 128 * half : 128 * half + 128] for k in range(8)], axis=0
            )
            at = pl.ds(pl.multiple_of(parity * 256 + 128 * half, 128), 128)
            for t in range(2):
                out_ref[t, :, at] = nn_dot(lefts[t], right)


def fc_weight_grad_of(place, flats, own, other):
    return pl.pallas_call(
        fc_weight_kernel,
        in_specs=[SMEM] + [VMEM] * 6,
        out_specs=VMEM,
        out_shape=jax.ShapeDtypeStruct((2, 576, 512), F32),
        compiler_params=params(SMALL),
        cost_estimate=cost(3e9, 5e6),
        name="fc_weight_grad",
    )(place, *flats, own, other)


def row_of(column):
    size = column.shape[0]
    eye = lax.broadcasted_iota(jnp.int32, (size, size), 0) == lax.broadcasted_iota(jnp.int32, (size, size), 1)
    return jnp.sum(jnp.where(eye, column, 0.0), axis=0, keepdims=True)


def total_kernel(part_0, part_1, part_2, part_3, conv_ref, bias_ref, first_ref, fc_bias_ref, second_ref):
    total = (part_0[...].astype(F32) + part_1[...].astype(F32)) + (part_2[...].astype(F32) + part_3[...].astype(F32))
    conv_ref[...] = total[0:288]
    for t in range(2):
        fc_bias_ref[t : t + 1] = total[288 + t : 289 + t, 0:256]
        bias_ref[t : t + 1] = row_of(total[288:304, 260 + t : 261 + t])
    for u in range(2):
        for v in range(2):
            line = 290 + 2 * u + v
            second_ref[u, v : v + 1] = total[line : line + 1, 0:256]
            place = 256 + u if u == v else 258 + v
            first_ref[u, v : v + 1] = row_of(total[288:304, place : place + 1])


def summed(parts):
    return pl.pallas_call(
        total_kernel,
        in_specs=[VMEM] * 4,
        out_specs=[VMEM] * 5,
        out_shape=[
            jax.ShapeDtypeStruct((288, 384), F32),
            jax.ShapeDtypeStruct((2, 16), F32),
            jax.ShapeDtypeStruct((2, 2, 16), F32),
            jax.ShapeDtypeStruct((2, 256), F32),
            jax.ShapeDtypeStruct((2, 2, 256), F32),
        ],
        compiler_params=params(SMALL),
        cost_estimate=cost(1e7, 3e6),
        name="summed",
    )(*parts)


def mp_moves(z_step, y_step, core_step):
    return [
        ((z * 4 + y) * 2 + c, (((z + z_step) % 2) * 4 + (y + y_step) % 4) * 2 + (c + core_step) % 2)
        for z in range(2)
        for y in range(4)
        for c in range(2)
    ]


def dp_moves(x_step, z_step):
    return [(x * 2 + h, ((x + x_step) % 4) * 2 + (h + z_step) % 2) for x in range(4) for h in range(2)]


SAME_CORE = [[2 * k + c for k in range(8)] for c in range(2)]
SAME_Z_CORE = [[8 * z + 2 * y + c for y in range(4)] for z in range(2) for c in range(2)]


def over_mp(array, z_step=0, y_step=0, core_step=0):
    return lax.ppermute(array, "mp", mp_moves(z_step, y_step, core_step))


def over_dp(array, x_step=0, z_step=0):
    return lax.ppermute(array, "dp", dp_moves(x_step, z_step))


def over_far_z(array):
    moves = [
        (((z * 4 + y) * 2 + c) * 8 + x * 2 + h, (((1 - z) * 4 + y) * 2 + c) * 8 + x * 2 + 1 - h)
        for z in range(2)
        for y in range(4)
        for c in range(2)
        for x in range(4)
        for h in range(2)
    ]
    return lax.ppermute(array, ("mp", "dp"), moves)


def dealt(array, groups=None, axis="mp"):
    return lax.all_to_all(array, axis, 0, 0, tiled=True, axis_index_groups=groups)


def pick(array, index, axis):
    return lax.dynamic_index_in_dim(array, index, axis, keepdims=False)


def local(
    inputs,
    conv_weight,
    conv_bias,
    first_stitch,
    fc_weight,
    fc_bias,
    second_stitch,
    crop_counts,
    out_grad,
):
    x = jnp.transpose(inputs, (0, 2, 3, 1, 4))
    kernels = jnp.transpose(conv_weight, (0, 1, 2, 4, 3)).reshape(2, 144, 384)
    stitch_one = jnp.transpose(first_stitch, (1, 2, 0))
    mp_at, dp_at = lax.axis_index("mp"), lax.axis_index("dp")
    z_at, y_at, core = mp_at // 8, (mp_at // 2) % 4, mp_at % 2
    x_at, h_at = dp_at // 2, dp_at % 2
    core_arg = core.astype(jnp.int32).reshape(1)

    column = [kernels] + [over_mp(kernels, y_step=k) for k in range(1, 4)]
    slope, pooled, flat_t, own, other = front(
        core_arg, x, fc_weight, kernels.reshape(288, 384), conv_bias, stitch_one
    )
    own, column = lax.optimization_barrier((own, column))
    own = pair_sum(own, over_mp(other, core_step=1))
    parts = dealt(own, SAME_CORE)

    flat_z = over_dp(flat_t, z_step=1)
    blocks_a, blocks_b = jnp.stack(column[0:2]), jnp.stack(column[2:4])
    far_a, far_b = over_mp(blocks_a, z_step=1), over_far_z(blocks_b)
    output, grad_copies, sums = hidden_layer(
        crop_counts,
        parts,
        fc_bias.T,
        jnp.transpose(second_stitch, (1, 2, 0)),
        jnp.transpose(out_grad, (1, 2, 0)),
    )
    grads_own = dealt(grad_copies, SAME_CORE)
    same = [blocks_a, blocks_b, far_a, far_b]
    kernels_all = turned(
        jnp.stack([core, z_at, y_at]).astype(jnp.int32), same + [over_mp(part, core_step=1) for part in same]
    )
    flat_pair = jnp.stack([flat_t, flat_z])
    flat_1, flat_3 = over_dp(flat_pair, x_step=1), over_dp(flat_pair, x_step=3)
    grads_own, flat_1, flat_3, kernels_all = lax.optimization_barrier((grads_own, flat_1, flat_3, kernels_all))
    grads_other = over_mp(grads_own, core_step=1)
    flat_2 = over_dp(flat_pair, x_step=2)
    slice_own = dealt(grads_own, axis="dp")
    send, pre, stats = back_fc(core_arg, grads_own, grads_other, fc_weight, stitch_one, pooled, slope)
    send, slice_own = lax.optimization_barrier((send, slice_own))
    slice_other = over_mp(slice_own, core_step=1)
    pre_all = dealt(send)

    weight_part = weight_grad(x, pre, sums, stats)
    weight_z = over_dp(weight_part, z_step=1)
    pre_all, weight_part = lax.optimization_barrier((pre_all, weight_part))
    input_part = input_grad_part(pre_all, kernels_all)
    input_part, weight_z, flat_2 = lax.optimization_barrier((input_part, weight_z, flat_2))
    flats = [flat_pair, flat_1, flat_3, flat_2]
    part = dealt(input_part)

    weight_pair = pair_sum(weight_part, weight_z)
    conv_sum, conv_bias_grad, first_sum, fc_bias_sum, second_sum = summed(
        [weight_pair] + [over_dp(weight_pair, x_step=k) for k in range(1, 4)]
    )
    crops_place = jnp.stack(
        [core] + [(x_at + 4 - k) % 4 * 2 + (h_at + dh) % 2 for k in (0, 1, 3, 2) for dh in range(2)]
    ).astype(jnp.int32)
    fc_weight_grad = fc_weight_grad_of(crops_place, flats, slice_own, slice_other)
    input_grad = jnp.transpose(placed_back(part), (0, 4, 1, 2, 3))

    conv_weight_grad = jnp.transpose(conv_sum.reshape(2, 3, 3, 16, 384), (0, 1, 2, 4, 3))
    first_stitch_grad = jnp.transpose(first_sum, (2, 0, 1))
    fc_bias_grad = fc_bias_sum.T
    second_stitch_grad = jnp.transpose(second_sum, (2, 0, 1))
    return (
        jnp.transpose(output, (2, 0, 1)),
        input_grad,
        conv_weight_grad,
        conv_bias_grad,
        first_stitch_grad,
        fc_weight_grad,
        fc_bias_grad,
        second_stitch_grad,
    )


def solution(mesh):
    placed = (
        P(None, "dp", None, None, None),
        P(None, None, None, None, "mp"),
        P(None, "mp"),
        P("mp", None, None),
        P(None, "mp", None),
        P("mp", None),
        P("mp", None, None),
        P("dp"),
        P("mp", None, "dp"),
    )
    return jax.shard_map(
        local,
        mesh=mesh,
        in_specs=placed,
        out_specs=(
            P("mp", None, "dp"),
            P(None, "dp", None, None, "mp"),
            P(None, None, None, None, "mp"),
            P(None, "mp"),
            P("mp", None, None),
            P(None, "mp", "dp"),
            P("mp", None),
            P("mp", None, None),
        ),
        check_vma=False,
    )
```

```python
import jax
import jax.numpy as jnp
from jax import lax
from jax.experimental import pallas as pl
from jax.experimental.pallas import tpu as pltpu
from jax.sharding import PartitionSpec as P

F32 = jnp.float32
BF16 = jnp.bfloat16
LARGE, MEDIUM, SMALL = 56, 50, 16


def params(mib=LARGE):
    return pltpu.CompilerParams(vmem_limit_bytes=mib * 1024 * 1024)


def cost(flops, read):
    return pl.CostEstimate(flops=int(flops), bytes_accessed=int(read), transcendentals=0)


def nt_dot(left, right):
    return lax.dot_general(left, right, (((1,), (1,)), ((), ())), preferred_element_type=F32)


def nn_dot(left, right):
    return lax.dot_general(left, right, (((1,), (0,)), ((), ())), preferred_element_type=F32)


def first_half(shape):
    return lax.broadcasted_iota(jnp.int32, shape, len(shape) - 1) < 64


def swap_halves(value):
    return pltpu.roll(value, 64, value.ndim - 1)


def gelu_parts(x):
    root, cubic = 0.7978845608028654, 0.044715
    square = x * x
    tanh = jnp.tanh(root * x * (1.0 + cubic * square))
    half = 0.5 + 0.5 * tanh
    slope = half + 0.5 * x * (1.0 - tanh * tanh) * (root * (1.0 + 3.0 * cubic * square))
    return x * half, slope


def spread(slabs):
    lane = lax.broadcasted_iota(jnp.int32, slabs[0].shape, 1)
    for bit in range(4):
        odd = (lane & (8 << bit)) != 0
        slabs = [jnp.where(odd, slabs[(k + (1 << bit)) % 16], slabs[k]) for k in range(16)]
    return slabs


def exchange(slabs):
    slabs = spread(slabs)
    slabs = [slabs[0]] + [pltpu.roll(slabs[k], 8 * k, 1) for k in range(1, 16)]
    slabs = spread(slabs)
    return [slabs[-k % 16] for k in range(16)]


def column(row):
    size = row.shape[1]
    eye = lax.broadcasted_iota(jnp.int32, (size, size), 0) == lax.broadcasted_iota(jnp.int32, (size, size), 1)
    return jnp.sum(jnp.where(eye, row, 0.0), axis=1, keepdims=True)


def by_tower(first, second):
    lead = first_half((16, 128))
    return jnp.where(lead, column(first), column(second))


def stitch_slabs(stitch_ref):
    part = [[stitch_ref[u, v : v + 1] for v in range(2)] for u in range(2)]
    own = by_tower(part[0][0], part[1][1])
    into = by_tower(part[0][1], part[1][0])
    back = by_tower(part[1][0], part[0][1])
    return own, into, back


def slab_order(fc_axis):
    fc_row = lax.broadcasted_iota(jnp.int32, (576, 576), fc_axis)
    slab_row = lax.broadcasted_iota(jnp.int32, (576, 576), 1 - fc_axis)
    return (fc_row == 36 * (slab_row & 15) + (slab_row >> 4)).astype(F32).astype(BF16)


def front_kernel(
    core_ref, x_ref, w_ref, kernel_ref, bias_ref, stitch_ref,
    slope_ref, pooled_ref, flat_t_ref, own_ref, other_ref,
    xs, ws, acc, ready, pool, slopes, pooled_out, flat_t_out, x_sem, w_sem, slope_sem, out_sem,
):
    def x_copy(i):
        return pltpu.make_async_copy(x_ref.at[:, i], xs.at[:, i], x_sem.at[i])

    def w_copy(t):
        return pltpu.make_async_copy(w_ref.at[t], ws.at[t], w_sem.at[t])

    def slope_copy(i):
        return pltpu.make_async_copy(slopes.at[i], slope_ref.at[i], slope_sem.at[i])

    for i in range(13):
        x_copy(i).start()
    for t in range(2):
        w_copy(t).start()
    acc[...] = jnp.zeros_like(acc)
    ready[...] = jnp.zeros_like(ready)
    pool[...] = jnp.zeros_like(pool)
    lead = first_half((16, 128))
    bias = by_tower(bias_ref[0:1], bias_ref[1:2])
    own, into, _ = stitch_slabs(stitch_ref)

    def gather(row):
        line = jnp.maximum(row + 1, 0)
        for t in range(2):
            right = pltpu.roll(acc[t, 0, line], 64, 1)
            left = pltpu.roll(acc[t, 2, line], 832, 1)
            ready[t] = acc[t, 1, line] + right + left

    def finish(row):
        acts = []
        for j in range(13):
            lanes = slice(j // 2 * 128, j // 2 * 128 + 128)
            zero, one = ready[0, :, lanes], ready[1, :, lanes]
            if j % 2 == 0:
                pre_act = jnp.where(lead, zero, swap_halves(one))
            else:
                pre_act = jnp.where(lead, swap_halves(zero), one)
            act, slope = gelu_parts(pre_act + bias)
            slopes[jnp.maximum(row, 0), j] = slope.astype(BF16)
            acts.append(act)
        even = row % 2 == 0
        for q in range(6):
            total = acts[2 * q] + acts[2 * q + 1] + acts[2 * q + 2]
            pool[jnp.maximum(row + 2, 0) // 2, q] += total
            pool[jnp.maximum(row, 0) // 2, q] += jnp.where(even, total, 0.0)

    def line(i, carry):
        x_copy(i).wait()
        finish(i - 3)
        gather(i - 2)
        for t in range(2):
            weights = kernel_ref[144 * t : 144 * t + 144]
            for start in range(0, 13, 4):
                width = min(4, 13 - start)
                rows = xs[t, i, start : start + width].reshape(64 * width, 384)
                product = nt_dot(weights, rows)
                for a in range(3):
                    for b in range(3):
                        top = 16 * (3 * a + b)
                        acc[t, b, i + 2 - a, :, 64 * start : 64 * (start + width)] += product[top : top + 16]
        return carry

    def last(i, carry):
        finish(i - 3)
        gather(jnp.minimum(i - 2, 12))
        return carry

    lax.fori_loop(0, 13, line, 0)
    lax.fori_loop(13, 16, last, 0)
    for i in range(13):
        slope_copy(i).start()
    pooled = pool[1:7].reshape(36, 16, 128) * (1.0 / 9.0)
    pooled_out[...] = pooled
    pooled_copy = pltpu.make_async_copy(pooled_out, pooled_ref, out_sem.at[0])
    pooled_copy.start()
    mixed = own[None] * pooled + into[None] * swap_halves(pooled)
    flat_t = nn_dot(slab_order(0), mixed.reshape(576, 128).astype(BF16))
    flat_t_out[...] = flat_t.astype(BF16)
    flat_copy = pltpu.make_async_copy(flat_t_out, flat_t_ref, out_sem.at[1])
    flat_copy.start()
    flat = flat_t.T.astype(BF16)
    core = core_ref[0]
    copies_out = [pooled_copy, flat_copy]
    for t in range(2):
        w_copy(t).wait()
    for ref, parity in ((other_ref, 1 - core), (own_ref, core)):
        for q in range(8):
            at = pl.ds(pl.multiple_of((2 * q + parity) * 256, 256), 256)
            for t in range(2):
                ref[q, 64 * t : 64 * t + 64] = nn_dot(flat[64 * t : 64 * t + 64], ws[t, :, at]).astype(BF16)
    for i in range(13):
        slope_copy(i).wait()
    for copy in copies_out:
        copy.wait()


VMEM = pl.BlockSpec(memory_space=pltpu.VMEM)
SMEM = pl.BlockSpec(memory_space=pltpu.SMEM)
ANY = pl.BlockSpec(memory_space=pl.ANY)


def front(core, x, w, kernels, bias, stitch):
    return pl.pallas_call(
        front_kernel,
        in_specs=[SMEM, ANY, ANY, VMEM, VMEM, VMEM],
        out_specs=[ANY, ANY, ANY, VMEM, VMEM],
        out_shape=[
            jax.ShapeDtypeStruct((13, 13, 16, 128), BF16),
            jax.ShapeDtypeStruct((36, 16, 128), F32),
            jax.ShapeDtypeStruct((576, 128), BF16),
            jax.ShapeDtypeStruct((8, 128, 256), BF16),
            jax.ShapeDtypeStruct((8, 128, 256), BF16),
        ],
        scratch_shapes=[
            pltpu.VMEM((2, 13, 13, 64, 384), BF16),
            pltpu.VMEM((2, 576, 4096), BF16),
            pltpu.VMEM((2, 3, 15, 16, 896), F32),
            pltpu.VMEM((2, 16, 896), F32),
            pltpu.VMEM((8, 6, 16, 128), F32),
            pltpu.VMEM((13, 13, 16, 128), BF16),
            pltpu.VMEM((36, 16, 128), F32),
            pltpu.VMEM((576, 128), BF16),
            pltpu.SemaphoreType.DMA((13,)),
            pltpu.SemaphoreType.DMA((2,)),
            pltpu.SemaphoreType.DMA((13,)),
            pltpu.SemaphoreType.DMA((2,)),
        ],
        compiler_params=params(),
        cost_estimate=cost(10e9, 30e6),
        name="front",
    )(core, x, w, kernels, bias, stitch)


def pair_kernel(first_ref, second_ref, out_ref):
    out_ref[...] = (first_ref[...].astype(F32) + second_ref[...].astype(F32)).astype(BF16)


def pair_sum(first, second):
    return pl.pallas_call(
        pair_kernel,
        in_specs=[VMEM, VMEM],
        out_specs=VMEM,
        out_shape=jax.ShapeDtypeStruct(first.shape, BF16),
        compiler_params=params(SMALL),
        cost_estimate=cost(1e6, 2e6),
        name="pair_sum",
    )(first, second)


def hidden_kernel(counts_ref, parts_ref, bias_ref, stitch_ref, cot_ref, out_ref, grad_ref, sums_ref):
    live = counts_ref[0]
    for k in range(1, 8):
        live += counts_ref[k]
    mask = (lax.broadcasted_iota(jnp.int32, (64, 256), 0) < live).astype(F32)
    total = parts_ref[0].astype(F32)
    for k in range(1, 8):
        total += parts_ref[k].astype(F32)
    hidden, slope = [], []
    for t in range(2):
        act, der = gelu_parts(total[64 * t : 64 * t + 64] + bias_ref[t][None])
        hidden.append(act)
        slope.append(der)
    cots = [cot_ref[u].astype(F32) * mask for u in range(2)]
    stitch = [[stitch_ref[u, v][None] for v in range(2)] for u in range(2)]
    sums = []
    for u in range(2):
        out_ref[u] = (mask * (stitch[u][0] * hidden[0] + stitch[u][1] * hidden[1])).astype(BF16)
    for v in range(2):
        grad = (stitch[0][v] * cots[0] + stitch[1][v] * cots[1]) * slope[v]
        grad = grad.astype(BF16)
        for k in range(8):
            for half in range(2):
                top = 128 * half + 64 * v
                grad_ref[k, top : top + 64] = grad[:, 128 * half : 128 * half + 128]
        sums.append(jnp.sum(grad.astype(F32), axis=0, keepdims=True))
    for u in range(2):
        for v in range(2):
            sums.append(jnp.sum(cots[u] * hidden[v], axis=0, keepdims=True))
    sums_ref[...] = jnp.concatenate(sums + [jnp.zeros((2, 256), F32)], axis=0)


def hidden_layer(counts, parts, bias, stitch, cot):
    vmem = pl.BlockSpec(memory_space=pltpu.VMEM)
    return pl.pallas_call(
        hidden_kernel,
        in_specs=[pl.BlockSpec(memory_space=pltpu.SMEM), vmem, vmem, vmem, vmem],
        out_specs=[vmem, vmem, vmem],
        out_shape=[
            jax.ShapeDtypeStruct((2, 64, 256), BF16),
            jax.ShapeDtypeStruct((8, 256, 128), BF16),
            jax.ShapeDtypeStruct((8, 256), F32),
        ],
        compiler_params=params(SMALL),
        cost_estimate=cost(1e7, 3e6),
        name="hidden_layer",
    )(counts, parts, bias, stitch, cot)


def back_kernel(
    core_ref, own_ref, other_ref, w_ref, stitch_ref, pooled_ref, slope_ref,
    send_ref, pre_ref, stats_ref,
    ws, pooled, slopes, sends, w_sem, in_sem, send_sem,
):
    def w_copy(k):
        at = pl.ds(1024 * k, 1024)
        return pltpu.make_async_copy(w_ref.at[:, :, at], ws.at[:, :, at], w_sem.at[k])

    later_in = [
        pltpu.make_async_copy(pooled_ref, pooled, in_sem.at[0]),
        pltpu.make_async_copy(slope_ref, slopes, in_sem.at[1]),
    ]
    for k in range(4):
        w_copy(k).start()
    for copy in later_in:
        copy.start()
    first = core_ref[0] == 0
    perm = slab_order(1)
    own_slab, _, back_slab = stitch_slabs(stitch_ref)
    totals = [jnp.zeros((576, 128), F32)] * 2
    for k in range(4):
        w_copy(k).wait()
        blocks = []
        for q in (2 * k, 2 * k + 1):
            own, other = (jnp.concatenate([ref[q, 0:128], ref[q, 128:256]], axis=1) for ref in (own_ref, other_ref))
            blocks += [jnp.where(first, own, other), jnp.where(first, other, own)]
        rows = jnp.concatenate(blocks, axis=1)
        for t in range(2):
            totals[t] = totals[t] + nt_dot(ws[t, :, 1024 * k : 1024 * k + 1024], rows)
    flat_grad = jnp.where(first_half((576, 128)), totals[0], totals[1])
    mixed_grad = nn_dot(perm, flat_grad.astype(BF16)).reshape(36, 16, 128)
    swapped = swap_halves(mixed_grad)
    pooled_grad = own_slab[None] * mixed_grad + back_slab[None] * swapped
    pooled_grad = (pooled_grad * (1.0 / 9.0)).reshape(6, 6, 16, 128)
    for copy in later_in:
        copy.wait()
    lead = first_half((16, 128))
    bias_sum = jnp.zeros((16, 128), F32)
    zero = jnp.zeros((16, 128), F32)
    widened = []
    for p in range(6):
        line = []
        for j in range(13):
            terms = [pooled_grad[p, q] for q in range(6) if 2 * q <= j <= 2 * q + 2]
            line.append(terms[0] if len(terms) == 1 else terms[0] + terms[1])
        widened.append(line)
    copies_out = []
    for i in range(13):
        windows = [p for p in range(6) if 2 * p <= i <= 2 * p + 2]
        slabs = []
        for j in range(13):
            value = widened[windows[0]][j]
            if len(windows) == 2:
                value = value + widened[windows[1]][j]
            value = (value * slopes[i, j].astype(F32)).astype(BF16)
            pre_ref[i, j] = value
            value = value.astype(F32)
            bias_sum = bias_sum + value
            slabs.append(value)
        slabs = exchange(slabs + [zero] * 3)
        at = pl.ds(128 * i, 128)
        for m in range(16):
            block = (m % 2) * 8 + m // 2
            sends[m, :, 128 * i : 128 * i + 128] = slabs[block].astype(BF16)
        copies_out.append(pltpu.make_async_copy(sends.at[:, :, at], send_ref.at[:, :, at], send_sem.at[i]))
        copies_out[-1].start()
    pooled_in = pooled[...]
    own = jnp.sum(mixed_grad * pooled_in, axis=0)
    cross = jnp.sum(swapped * pooled_in, axis=0)
    lane = lax.broadcasted_iota(jnp.int32, (16, 128), 1)
    stats = jnp.zeros((16, 128), F32)
    for k, value in enumerate((own, cross, bias_sum)):
        for t in range(2):
            half = jnp.sum(jnp.where(lead == (t == 0), value, 0.0), axis=1, keepdims=True)
            stats = jnp.where(lane == 2 * k + t, half, stats)
    stats_ref[...] = stats
    for copy in copies_out:
        copy.wait()


def back_fc(core, own, other, w, stitch, pooled, slope):
    return pl.pallas_call(
        back_kernel,
        in_specs=[SMEM, VMEM, VMEM, ANY, VMEM, ANY, ANY],
        out_specs=[ANY, VMEM, VMEM],
        out_shape=[
            jax.ShapeDtypeStruct((16, 16, 1664), BF16),
            jax.ShapeDtypeStruct((13, 13, 16, 128), BF16),
            jax.ShapeDtypeStruct((16, 128), F32),
        ],
        scratch_shapes=[
            pltpu.VMEM((2, 576, 4096), BF16),
            pltpu.VMEM((36, 16, 128), F32),
            pltpu.VMEM((13, 13, 16, 128), BF16),
            pltpu.VMEM((16, 16, 1664), BF16),
            pltpu.SemaphoreType.DMA((4,)),
            pltpu.SemaphoreType.DMA((2,)),
            pltpu.SemaphoreType.DMA((13,)),
        ],
        compiler_params=params(),
        cost_estimate=cost(1e9, 30e6),
        name="back_fc",
    )(core, own, other, w, stitch, pooled, slope)


def weight_kernel(x_ref, pre_ref, sums_ref, stats_ref, out_ref, xs, lines, acc, x_sem):
    def x_copy(i):
        return pltpu.make_async_copy(x_ref.at[:, i], xs.at[:, i], x_sem.at[i])

    for i in range(13):
        x_copy(i).start()
    lines[...] = jnp.zeros_like(lines)
    acc[...] = jnp.zeros_like(acc)
    lead = first_half((16, 128))

    def merge(i, carry):
        zero = jnp.zeros((16, 128), F32)
        slabs = [pre_ref[i, j].astype(F32) for j in range(13)]
        turned = [swap_halves(slab) for slab in slabs]
        slabs = [zero] + slabs + [zero] * 2
        turned = [zero] + turned + [zero] * 2
        for first in range(-1, 14):
            left, right = first + 1, first + 2
            pair = (
                jnp.where(lead, slabs[left], turned[right]).astype(BF16),
                jnp.where(lead, turned[left], slabs[right]).astype(BF16),
            )
            for b in range(3):
                place = first + b - 1
                if place % 2 == 0 and 0 <= place <= 12:
                    for t in range(2):
                        lines[t, b, i + 1, :, 64 * place : 64 * place + 128] = pair[t]
        return carry

    lax.fori_loop(0, 13, merge, 0)

    def line(i, carry):
        x_copy(i).wait()
        for t in range(2):
            left = jnp.concatenate([lines[t, b, i + 2 - a] for a in range(3) for b in range(3)], axis=0)
            right = jnp.concatenate([xs[t, i].reshape(832, 384), jnp.zeros((64, 384), BF16)], axis=0)
            acc[144 * t : 144 * t + 144] += nn_dot(left, right)
        return carry

    lax.fori_loop(0, 13, line, 0)
    out_ref[0:288] = acc[...].astype(BF16)
    small = jnp.concatenate([sums_ref[...], jnp.zeros((8, 256), F32)], axis=0)
    out_ref[288:304] = jnp.concatenate([small, stats_ref[...]], axis=1).astype(BF16)


def weight_grad(x, pre, sums, stats):
    return pl.pallas_call(
        weight_kernel,
        in_specs=[ANY, VMEM, VMEM, VMEM],
        out_specs=VMEM,
        out_shape=jax.ShapeDtypeStruct((304, 384), BF16),
        scratch_shapes=[
            pltpu.VMEM((2, 13, 13, 64, 384), BF16),
            pltpu.VMEM((2, 3, 15, 16, 896), BF16),
            pltpu.VMEM((288, 384), F32),
            pltpu.SemaphoreType.DMA((13,)),
        ],
        compiler_params=params(MEDIUM),
        cost_estimate=cost(10e9, 20e6),
        name="weight_grad",
    )(x, pre, sums, stats)


def turn_kernel(place_ref, *refs):
    out_ref, rows = refs[8:]
    core, z, y = place_ref[0], place_ref[1], place_ref[2]
    for parity, group in ((core, refs[0:4]), (1 - core, refs[4:8])):
        for part, ref in enumerate(group):
            for k in range(2):
                from_y = lax.rem(y + 4 - (2 * (part % 2) + k), 4)
                block = 8 * (z if part < 2 else 1 - z) + 2 * from_y + parity
                at = pl.ds(pl.multiple_of(16 * block, 16), 16)
                for tap in range(9):
                    rows[tap, at] = ref[k, core, 16 * tap : 16 * tap + 16]
    for tap in range(9):
        out_ref[:, 256 * tap : 256 * tap + 256] = rows[tap].T


def turned(place, parts):
    return pl.pallas_call(
        turn_kernel,
        in_specs=[SMEM] + [VMEM] * 8,
        out_specs=VMEM,
        out_shape=jax.ShapeDtypeStruct((384, 2304), BF16),
        scratch_shapes=[pltpu.VMEM((9, 256, 384), BF16)],
        compiler_params=params(63),
        cost_estimate=cost(1e9, 4e6),
        name="turned_kernels",
    )(place, *parts)


def input_kernel(g_ref, w_ref, out_ref, taps):
    zero = jnp.zeros((256, 128), BF16)
    for b in range(3):
        taps[b, :, 0:128] = zero
        taps[b, :, 1792:1920] = zero

    def widen(i):
        row = g_ref[:, :, 128 * i : 128 * i + 128].reshape(256, 128)
        at = slice(128 * i + 128, 128 * i + 256)
        taps[1, :, at] = row
        row = row.astype(F32)
        taps[0, :, at] = pltpu.roll(row, 120, 1).astype(BF16)
        taps[2, :, at] = pltpu.roll(row, 8, 1).astype(BF16)

    for i in range(3):
        widen(i)
    weights = w_ref[...]
    for start in range(0, 13, 2):
        width = 128 * min(2, 13 - start)
        right = jnp.concatenate(
            [
                taps[b, :, 128 * (start + 2 - a) : 128 * (start + 2 - a) + width]
                for a in range(3)
                for b in range(3)
            ],
            axis=0,
        )
        for i in range(start + 3, min(start + 5, 13)):
            widen(i)
        product = nn_dot(weights, right)
        for m in range(16):
            out_ref[m, :, 128 * start : 128 * start + width] = product[24 * m : 24 * m + 24].astype(BF16)


def input_grad_part(g, w):
    return pl.pallas_call(
        input_kernel,
        in_specs=[VMEM, VMEM],
        out_specs=VMEM,
        out_shape=jax.ShapeDtypeStruct((16, 24, 1664), BF16),
        scratch_shapes=[pltpu.VMEM((3, 256, 1920), BF16)],
        compiler_params=params(SMALL),
        cost_estimate=cost(4e9, 20e6),
        name="input_grad",
    )(g, w)


def place_kernel(part_ref, out_ref, rows, sem):
    copies = [pltpu.make_async_copy(rows.at[:, i], out_ref.at[:, i], sem.at[i]) for i in range(13)]
    for i in range(13):
        lanes = slice(128 * i, 128 * i + 128)
        slabs = [part_ref[2 * (block % 8) + block // 8, :, lanes].astype(F32) for block in range(16)]
        slabs = exchange(slabs)
        for j in range(13):
            rows[0, i, j] = slabs[j][:, 0:64].astype(BF16)
            rows[1, i, j] = swap_halves(slabs[j])[:, 0:64].astype(BF16)
        copies[i].start()
    for copy in copies:
        copy.wait()


def placed_back(parts):
    return pl.pallas_call(
        place_kernel,
        in_specs=[VMEM],
        out_specs=ANY,
        out_shape=jax.ShapeDtypeStruct((2, 13, 13, 24, 64), BF16),
        scratch_shapes=[pltpu.VMEM((2, 13, 13, 24, 64), BF16), pltpu.SemaphoreType.DMA((13,))],
        compiler_params=params(SMALL),
        cost_estimate=cost(1e8, 3e6),
        name="placed_back",
    )(parts)


def fc_weight_kernel(place_ref, flat_0, flat_1, flat_3, flat_2, own_ref, other_ref, out_ref):
    core = place_ref[0]
    lead = first_half((576, 128))
    zero = jnp.zeros((576, 128), BF16)
    flats = [ref[h] for ref in (flat_0, flat_1, flat_3, flat_2) for h in range(2)]
    lefts = [
        jnp.concatenate([jnp.where(lead, flat, zero) for flat in flats], axis=1),
        jnp.concatenate([jnp.where(lead, zero, flat) for flat in flats], axis=1),
    ]
    for ref, parity in ((own_ref, core), (other_ref, 1 - core)):
        for half in range(2):
            right = jnp.concatenate(
                [ref[place_ref[1 + k], 128 * half : 128 * half + 128] for k in range(8)], axis=0
            )
            at = pl.ds(pl.multiple_of(parity * 256 + 128 * half, 128), 128)
            for t in range(2):
                out_ref[t, :, at] = nn_dot(lefts[t], right)


def fc_weight_grad_of(place, flats, own, other):
    return pl.pallas_call(
        fc_weight_kernel,
        in_specs=[SMEM] + [VMEM] * 6,
        out_specs=VMEM,
        out_shape=jax.ShapeDtypeStruct((2, 576, 512), F32),
        compiler_params=params(SMALL),
        cost_estimate=cost(3e9, 5e6),
        name="fc_weight_grad",
    )(place, *flats, own, other)


def row_of(column):
    size = column.shape[0]
    eye = lax.broadcasted_iota(jnp.int32, (size, size), 0) == lax.broadcasted_iota(jnp.int32, (size, size), 1)
    return jnp.sum(jnp.where(eye, column, 0.0), axis=0, keepdims=True)


def total_kernel(part_0, part_1, part_2, part_3, conv_ref, bias_ref, first_ref, fc_bias_ref, second_ref):
    total = (part_0[...].astype(F32) + part_1[...].astype(F32)) + (part_2[...].astype(F32) + part_3[...].astype(F32))
    conv_ref[...] = total[0:288]
    for t in range(2):
        fc_bias_ref[t : t + 1] = total[288 + t : 289 + t, 0:256]
        bias_ref[t : t + 1] = row_of(total[288:304, 260 + t : 261 + t])
    for u in range(2):
        for v in range(2):
            line = 290 + 2 * u + v
            second_ref[u, v : v + 1] = total[line : line + 1, 0:256]
            place = 256 + u if u == v else 258 + v
            first_ref[u, v : v + 1] = row_of(total[288:304, place : place + 1])


def summed(parts):
    return pl.pallas_call(
        total_kernel,
        in_specs=[VMEM] * 4,
        out_specs=[VMEM] * 5,
        out_shape=[
            jax.ShapeDtypeStruct((288, 384), F32),
            jax.ShapeDtypeStruct((2, 16), F32),
            jax.ShapeDtypeStruct((2, 2, 16), F32),
            jax.ShapeDtypeStruct((2, 256), F32),
            jax.ShapeDtypeStruct((2, 2, 256), F32),
        ],
        compiler_params=params(SMALL),
        cost_estimate=cost(1e7, 3e6),
        name="summed",
    )(*parts)


def mp_moves(z_step, y_step, core_step):
    return [
        ((z * 4 + y) * 2 + c, (((z + z_step) % 2) * 4 + (y + y_step) % 4) * 2 + (c + core_step) % 2)
        for z in range(2)
        for y in range(4)
        for c in range(2)
    ]


def dp_moves(x_step, z_step):
    return [(x * 2 + h, ((x + x_step) % 4) * 2 + (h + z_step) % 2) for x in range(4) for h in range(2)]


SAME_CORE = [[2 * k + c for k in range(8)] for c in range(2)]
SAME_Z_CORE = [[8 * z + 2 * y + c for y in range(4)] for z in range(2) for c in range(2)]


def over_mp(array, z_step=0, y_step=0, core_step=0):
    return lax.ppermute(array, "mp", mp_moves(z_step, y_step, core_step))


def over_dp(array, x_step=0, z_step=0):
    return lax.ppermute(array, "dp", dp_moves(x_step, z_step))


def over_far_z(array):
    moves = [
        (((z * 4 + y) * 2 + c) * 8 + x * 2 + h, (((1 - z) * 4 + y) * 2 + c) * 8 + x * 2 + 1 - h)
        for z in range(2)
        for y in range(4)
        for c in range(2)
        for x in range(4)
        for h in range(2)
    ]
    return lax.ppermute(array, ("mp", "dp"), moves)


def dealt(array, groups=None, axis="mp"):
    return lax.all_to_all(array, axis, 0, 0, tiled=True, axis_index_groups=groups)


def pick(array, index, axis):
    return lax.dynamic_index_in_dim(array, index, axis, keepdims=False)


def local(
    inputs,
    conv_weight,
    conv_bias,
    first_stitch,
    fc_weight,
    fc_bias,
    second_stitch,
    crop_counts,
    out_grad,
):
    x = jnp.transpose(inputs, (0, 2, 3, 1, 4))
    kernels = jnp.transpose(conv_weight, (0, 1, 2, 4, 3)).reshape(2, 144, 384)
    stitch_one = jnp.transpose(first_stitch, (1, 2, 0))
    mp_at, dp_at = lax.axis_index("mp"), lax.axis_index("dp")
    z_at, y_at, core = mp_at // 8, (mp_at // 2) % 4, mp_at % 2
    x_at, h_at = dp_at // 2, dp_at % 2
    core_arg = core.astype(jnp.int32).reshape(1)

    column = [kernels] + [over_mp(kernels, y_step=k) for k in range(1, 4)]
    slope, pooled, flat_t, own, other = front(
        core_arg, x, fc_weight, kernels.reshape(288, 384), conv_bias, stitch_one
    )
    own, column = lax.optimization_barrier((own, column))
    own = pair_sum(own, over_mp(other, core_step=1))
    parts = dealt(own, SAME_CORE)

    flat_z = over_dp(flat_t, z_step=1)
    blocks_a, blocks_b = jnp.stack(column[0:2]), jnp.stack(column[2:4])
    far_a, far_b = over_mp(blocks_a, z_step=1), over_far_z(blocks_b)
    output, grad_copies, sums = hidden_layer(
        crop_counts,
        parts,
        fc_bias.T,
        jnp.transpose(second_stitch, (1, 2, 0)),
        jnp.transpose(out_grad, (1, 2, 0)),
    )
    grads_own = dealt(grad_copies, SAME_CORE)
    same = [blocks_a, blocks_b, far_a, far_b]
    kernels_all = turned(
        jnp.stack([core, z_at, y_at]).astype(jnp.int32), same + [over_mp(part, core_step=1) for part in same]
    )
    flat_pair = jnp.stack([flat_t, flat_z])
    flat_1, flat_3 = over_dp(flat_pair, x_step=1), over_dp(flat_pair, x_step=3)
    grads_own, flat_1, flat_3, kernels_all = lax.optimization_barrier((grads_own, flat_1, flat_3, kernels_all))
    grads_other = over_mp(grads_own, core_step=1)
    flat_2 = over_dp(flat_pair, x_step=2)
    slice_own = dealt(grads_own, axis="dp")
    send, pre, stats = back_fc(core_arg, grads_own, grads_other, fc_weight, stitch_one, pooled, slope)
    send, slice_own = lax.optimization_barrier((send, slice_own))
    slice_other = over_mp(slice_own, core_step=1)
    pre_all = dealt(send)

    weight_part = weight_grad(x, pre, sums, stats)
    weight_z = over_dp(weight_part, z_step=1)
    pre_all, weight_part = lax.optimization_barrier((pre_all, weight_part))
    input_part = input_grad_part(pre_all, kernels_all)
    input_part, weight_z, flat_2 = lax.optimization_barrier((input_part, weight_z, flat_2))
    flats = [flat_pair, flat_1, flat_3, flat_2]
    part = dealt(input_part)

    weight_pair = pair_sum(weight_part, weight_z)
    conv_sum, conv_bias_grad, first_sum, fc_bias_sum, second_sum = summed(
        [weight_pair] + [over_dp(weight_pair, x_step=k) for k in range(1, 4)]
    )
    crops_place = jnp.stack(
        [core] + [(x_at + 4 - k) % 4 * 2 + (h_at + dh) % 2 for k in (0, 1, 3, 2) for dh in range(2)]
    ).astype(jnp.int32)
    fc_weight_grad = fc_weight_grad_of(crops_place, flats, slice_own, slice_other)
    input_grad = jnp.transpose(placed_back(part), (0, 4, 1, 2, 3))

    conv_weight_grad = jnp.transpose(conv_sum.reshape(2, 3, 3, 16, 384), (0, 1, 2, 4, 3))
    first_stitch_grad = jnp.transpose(first_sum, (2, 0, 1))
    fc_bias_grad = fc_bias_sum.T
    second_stitch_grad = jnp.transpose(second_sum, (2, 0, 1))
    return (
        jnp.transpose(output, (2, 0, 1)),
        input_grad,
        conv_weight_grad,
        conv_bias_grad,
        first_stitch_grad,
        fc_weight_grad,
        fc_bias_grad,
        second_stitch_grad,
    )


def solution(mesh):
    placed = (
        P(None, "dp", None, None, None),
        P(None, None, None, None, "mp"),
        P(None, "mp"),
        P("mp", None, None),
        P(None, "mp", None),
        P("mp", None),
        P("mp", None, None),
        P("dp"),
        P("mp", None, "dp"),
    )
    return jax.shard_map(
        local,
        mesh=mesh,
        in_specs=placed,
        out_specs=(
            P("mp", None, "dp"),
            P(None, "dp", None, None, "mp"),
            P(None, None, None, None, "mp"),
            P(None, "mp"),
            P("mp", None, None),
            P(None, "mp", "dp"),
            P("mp", None),
            P("mp", None, None),
        ),
        check_vma=False,
    )
```
